256 devices in a mesh: dp: 64 (over x_hi, z, y), tensor: 4 (over x_lo, core).
Axes of the slice: x: 4 (x_hi: 2, x_lo: 2; x = x_hi * 2 + x_lo), y: 4, z: 8, core: 2. Of those that a mesh axis runs over, the one named last changes fastest.
Arguments:
- queries: bfloat16 [32768, 4096], P('dp', 'tensor'), may hold values from -400 to 400
- keys: bfloat16 [32768, 4096], P('dp', 'tensor'), may hold values from -4 to 4
- values: bfloat16 [32768, 4096], P('dp', 'tensor'), may hold values from -6 to 6
- out_grad: bfloat16 [32768, 4096], P('dp', 'tensor'), may hold values from -6 to 6
- layer_input: bfloat16 [32768, 4096], P('dp', 'tensor'), may hold values from -6 to 6
- gate_weight: bfloat16 [4096, 32], P('tensor'), may hold values from -0.09375 to 0.09375
- gate_bias: float32 [32], P('tensor'), may hold values from 3.5 to 10
- doc_lengths: int32 [64], replicated, may hold values from 1 to 1024, 32768 in all
Outputs:
- query_grad: bfloat16 [32768, 4096], P('dp', 'tensor')
- key_grad: bfloat16 [32768, 4096], P('dp', 'tensor')
- value_grad: bfloat16 [32768, 4096], P('dp', 'tensor')
- weight_grad: float32 [4096, 32], P('tensor')
- bias_grad: float32 [32], P('tensor')
The draws below stay inside these ranges and needn't reach their ends.
Inputs may be any that keep to these rules, and one draw needn't show every extreme that they name: `doc_lengths`: the lengths sum to 32768; the longest document has exactly 1024 tokens.
All inputs are finite; a program needn't handle non-finite values.
Results may differ from the reference program's by a relative error of at most 0.0062.
Values may be sent and summed in bfloat16 or wider, within the bound.
A program may use at most 192 MiB of HBM per device.

```python
import math
import jax
import jax.numpy as jnp
import numpy as np
from jax import lax

D = 4096
HEADS = 32
HEAD_DIM = 128
TOK_DEV = 512
SPAN = 2
TOKENS = 32768
DOCS = 64
DOC_MOST = 1024
N_DP = 64


def shared_keys(key):
    return jnp.clip(jax.random.normal(key, (TOKENS, HEADS * HEAD_DIM), jnp.float32), -4.0, 4.0)


def draw_keys(key, part):
    return shared_keys(key).astype(jnp.bfloat16)


def draw_queries(key, part):
    key = jax.random.fold_in(key, 11)
    drawn = jnp.clip(jax.random.normal(key, (TOKENS, HEADS * HEAD_DIM), jnp.float32), -4.0, 4.0)
    return drawn.astype(jnp.bfloat16)


def level_of(rng, dims, cuts, smallest, largest):
    def one(dim, shards_of):
        heights = jax.random.uniform(jax.random.fold_in(jax.random.fold_in(rng, 6), dim), (shards_of,), jnp.float32, smallest / len(cuts), largest / len(cuts))
        return jnp.repeat(jnp.exp(heights), dims[dim] // shards_of).reshape((-1,) + (1,) * (len(dims) - dim - 1))

    loudness = one(*cuts[0])
    for cut in cuts[1:]:
        loudness = loudness * one(*cut)
    return loudness


def profile(number_of, total, most, slope):
    portions = [(1 << 20) // math.isqrt(grade ** slope) + 1 for grade in range(2, number_of + 1)]
    rest, given = total - most - (number_of - 1), [1] * (number_of - 1)
    while rest > 0:
        candidates = [i for i in range(number_of - 1) if given[i] < most]
        whole, left = sum([portions[i] for i in candidates]), rest
        for i in candidates:
            extra = min(most - given[i], max(1, left * portions[i] // whole), rest)
            given[i] = given[i] + extra
            rest = rest - extra
    return np.array([most] + given)


def uneven(stream_key, amount, total, reach, slope):
    if amount == 2:
        one = jax.random.randint(stream_key, (), max(1, total - reach), min(reach, total - 1) + 1)
        return jnp.stack([one, total - one])
    lengths = jnp.asarray(profile(amount, total, reach, slope), jnp.int32)
    pairs = (amount - 1) // 2
    source_of, receiver = lengths[1:1 + 2 * pairs:2], lengths[2:2 + 2 * pairs:2]
    room = jnp.minimum(source_of - 1, reach - receiver)
    shifted = jax.random.randint(jax.random.fold_in(stream_key, 1), (pairs,), 0, 1 << 20) % (room + 1)
    lengths = lengths.at[1:1 + 2 * pairs:2].set(source_of - shifted).at[2:2 + 2 * pairs:2].set(receiver + shifted)
    return lengths[jax.random.permutation(jax.random.fold_in(stream_key, 2), amount)]


def bell_draw(stream_key, extent, deviation, limit, cuts=(), kind=jnp.bfloat16):
    drawn = jax.random.normal(stream_key, extent, jnp.float32) * deviation
    if len(cuts) > 0:
        drawn = level_of(stream_key, extent, cuts, -0.22, 0.18) * drawn
    return jnp.clip(drawn, min=-limit, max=limit).astype(kind)


def setup_inputs(seed: int = 0) -> dict:
    seeds = jax.random.split(jax.random.key(seed), 9)
    return {
        "queries": draw_queries(jax.random.fold_in(seeds[8], 71), 0),
        "keys": draw_keys(jax.random.fold_in(seeds[8], 71), 0),
        "values": bell_draw(seeds[2], (TOKENS, HEADS * HEAD_DIM), 1.0, 6.0, ((0, 64), (1, 4))),
        "out_grad": bell_draw(seeds[3], (TOKENS, HEADS * HEAD_DIM), 1.0, 6.0, ((0, 64), (1, 4))),
        "layer_input": bell_draw(seeds[4], (TOKENS, D), 1.0, 6.0, ((0, 64), (1, 4))),
        "gate_weight": bell_draw(seeds[5], (D, HEADS), D ** -0.5, 0.09375, ((0, 4),)),
        "gate_bias": jnp.clip(3.5 + 6.5 * jax.random.uniform(seeds[6], (HEADS,), jnp.float32) ** level_of(seeds[6], (HEADS,), ((0, 4),), -0.2, 0.2), 3.5, 10.0),
        "doc_lengths": uneven(seeds[7], DOCS, TOKENS, DOC_MOST, 1).astype(jnp.int32),
    }


def round_trip(array):
    return lax.optimization_barrier(array.astype(jnp.bfloat16)).astype(jnp.float32)


def head_terms(query_cols, key_cols, value_cols, grad_cols, decay_rows, decay_keys, live_pairs, blocks, shard_rows):
    scale = HEAD_DIM ** -0.5
    row_count = query_cols.shape[0]
    score = jnp.dot(query_cols, key_cols.T, preferred_element_type=jnp.float32) * scale + decay_rows[:, None] - decay_keys[None, :]
    masked = jnp.where(live_pairs, score, -1e30)
    grouped = masked.reshape(row_count, blocks, shard_rows)
    live_grouped = live_pairs.reshape(row_count, blocks, shard_rows)
    block_top = jnp.max(grouped, axis=2)
    block_unscaled = jnp.where(live_grouped, jnp.exp(grouped - block_top[:, :, None]), 0.0)
    block_sum = jnp.sum(block_unscaled, axis=2)
    block_weight_tile = round_trip(block_unscaled)
    value_block_list = value_cols.reshape(blocks, shard_rows, HEAD_DIM).astype(jnp.float32)
    block_output_tile = jnp.einsum("lon,onu->lou", block_weight_tile, value_block_list)
    row_peak = jnp.max(block_top, axis=1)
    rescale = jnp.exp(block_top - row_peak[:, None])
    row_total = jnp.sum(block_sum * rescale, axis=1)
    attended = jnp.sum(block_output_tile * rescale[:, :, None], axis=1) / row_total[:, None]
    log_total = row_peak + jnp.log(row_total)
    row_delta = jnp.sum(grad_cols.astype(jnp.float32) * attended, axis=1)
    prob = jnp.where(live_pairs, jnp.exp(masked - log_total[:, None]), 0.0)
    prob_grad = jnp.dot(grad_cols, value_cols.T, preferred_element_type=jnp.float32)
    score_grad = prob * (prob_grad - row_delta[:, None])
    score_low = score_grad.astype(jnp.bfloat16)
    prob_low = prob.astype(jnp.bfloat16)
    query_part = jnp.dot(score_low, key_cols, preferred_element_type=jnp.float32) * scale
    key_part = jnp.dot(score_low.T, query_cols, preferred_element_type=jnp.float32) * scale
    value_part = jnp.dot(prob_low.T, grad_cols, preferred_element_type=jnp.float32)
    return query_part, key_part, value_part, jnp.sum(score_grad, axis=1), jnp.sum(score_grad, axis=0)


def reference(queries, keys, values, out_grad, layer_input, gate_weight, gate_bias, doc_lengths):
    feature_width = HEADS * HEAD_DIM
    gate_logit = jnp.dot(layer_input, gate_weight, preferred_element_type=jnp.float32) + gate_bias
    log_keep = jax.nn.log_sigmoid(gate_logit)
    decay = jnp.cumsum(log_keep, axis=0)
    doc_ends = jnp.cumsum(doc_lengths).astype(jnp.int32)
    positions = jnp.arange(TOKENS, dtype=jnp.int32)
    doc_ids = jnp.sum((positions[:, None] >= doc_ends[None, :]).astype(jnp.int32), axis=1)
    margin = SPAN * TOK_DEV
    window = margin + TOK_DEV
    key_pad = jnp.concatenate([jnp.zeros((margin, feature_width), keys.dtype), keys])
    value_pad = jnp.concatenate([jnp.zeros((margin, feature_width), values.dtype), values])
    decay_pad = jnp.concatenate([jnp.zeros((margin, HEADS), jnp.float32), decay])
    doc_pad = jnp.concatenate([jnp.full((margin,), -1, jnp.int32), doc_ids])
    pos_pad = jnp.arange(-margin, TOKENS, dtype=jnp.int32)
    remote_rows = jnp.arange(window, dtype=jnp.int32) < margin

    def block_step(totals_carry, block_index):
        key_acc, value_acc, col_acc = totals_carry
        row_start = (block_index * TOK_DEV).astype(jnp.int32)
        query_block = lax.dynamic_slice_in_dim(queries, row_start, TOK_DEV, 0)
        grad_block = lax.dynamic_slice_in_dim(out_grad, row_start, TOK_DEV, 0)
        decay_block = lax.dynamic_slice_in_dim(decay, row_start, TOK_DEV, 0)
        doc_block = lax.dynamic_slice_in_dim(doc_ids, row_start, TOK_DEV, 0)
        pos_block = lax.dynamic_slice_in_dim(positions, row_start, TOK_DEV, 0)
        key_window = lax.dynamic_slice_in_dim(key_pad, row_start, window, 0)
        value_window = lax.dynamic_slice_in_dim(value_pad, row_start, window, 0)
        decay_window = lax.dynamic_slice_in_dim(decay_pad, row_start, window, 0)
        doc_window = lax.dynamic_slice_in_dim(doc_pad, row_start, window, 0)
        pos_window = lax.dynamic_slice_in_dim(pos_pad, row_start, window, 0)
        live_pairs = (doc_block[:, None] == doc_window[None, :]) & (pos_window[None, :] <= pos_block[:, None])

        def one_head(head_index):
            first_col = head_index * HEAD_DIM
            return head_terms(
                lax.dynamic_slice_in_dim(query_block, first_col, HEAD_DIM, 1),
                lax.dynamic_slice_in_dim(key_window, first_col, HEAD_DIM, 1),
                lax.dynamic_slice_in_dim(value_window, first_col, HEAD_DIM, 1),
                lax.dynamic_slice_in_dim(grad_block, first_col, HEAD_DIM, 1),
                lax.dynamic_slice_in_dim(decay_block, head_index, 1, 1)[:, 0],
                lax.dynamic_slice_in_dim(decay_window, head_index, 1, 1)[:, 0],
                live_pairs, SPAN + 1, TOK_DEV)

        query_part, key_part, value_part, row_sum, col_sum = lax.map(one_head, jnp.arange(HEADS, dtype=jnp.int32))
        query_part = query_part.transpose(1, 0, 2).reshape(TOK_DEV, feature_width)
        key_part = key_part.transpose(1, 0, 2).reshape(window, feature_width)
        value_part = value_part.transpose(1, 0, 2).reshape(window, feature_width)
        key_part = jnp.where(remote_rows[:, None], round_trip(key_part), key_part)
        value_part = jnp.where(remote_rows[:, None], round_trip(value_part), value_part)
        key_acc = lax.dynamic_update_slice_in_dim(key_acc, lax.dynamic_slice_in_dim(key_acc, row_start, window, 0) + key_part, row_start, 0)
        value_acc = lax.dynamic_update_slice_in_dim(value_acc, lax.dynamic_slice_in_dim(value_acc, row_start, window, 0) + value_part, row_start, 0)
        col_acc = lax.dynamic_update_slice_in_dim(col_acc, lax.dynamic_slice_in_dim(col_acc, row_start, window, 0) + col_sum.T, row_start, 0)
        return (key_acc, value_acc, col_acc), (query_part, row_sum.T)

    start_carry = (jnp.zeros((margin + TOKENS, feature_width), jnp.float32),
                   jnp.zeros((margin + TOKENS, feature_width), jnp.float32),
                   jnp.zeros((margin + TOKENS, HEADS), jnp.float32))
    final_carry, stacked = lax.scan(block_step, start_carry, jnp.arange(N_DP, dtype=jnp.int32))
    key_acc, value_acc, col_acc = final_carry
    query_blocks, row_blocks = stacked
    query_grad = query_blocks.reshape(TOKENS, feature_width).astype(jnp.bfloat16)
    key_grad = key_acc[margin:].astype(jnp.bfloat16)
    value_grad = value_acc[margin:].astype(jnp.bfloat16)
    decay_grad = row_blocks.reshape(TOKENS, HEADS) - col_acc[margin:]
    keep_grad = jnp.flip(jnp.cumsum(jnp.flip(decay_grad, 0), axis=0), 0)
    gate_grad = keep_grad * jax.nn.sigmoid(-gate_logit)
    weight_grad = jnp.dot(layer_input.T, gate_grad.astype(jnp.bfloat16), preferred_element_type=jnp.float32)
    bias_grad = jnp.sum(gate_grad, axis=0)
    return query_grad, key_grad, value_grad, weight_grad, bias_grad
```

```python
import functools
import math

import jax
import jax.numpy as jnp
from jax import lax
from jax.experimental import pallas as pl
from jax.experimental.pallas import tpu as pltpu
from jax.sharding import PartitionSpec as P

RING = 4
HALO = 1024
HEAD = 128
TILE = 256
BAND = HALO + TILE
LOG2E = math.log2(math.e)
DEAD = -1e30
MESH = pl.DeviceIdType.MESH
F32 = jnp.float32
BF16 = jnp.bfloat16


def place():
    dp, tensor = lax.axis_index("dp"), lax.axis_index("tensor")
    y = lax.rem(dp, RING)
    return dp, tensor, y, dp - y


def ring_peer(dp, y, step):
    return dp - y + lax.rem(y + step, RING)


def greet(devices):
    barrier = pltpu.get_barrier_semaphore()
    for device in devices:
        pl.semaphore_signal(barrier, inc=1, device_id=device, device_id_type=MESH)
    pl.semaphore_wait(barrier, len(devices))


def send(src, dst, sems, at, device):
    copy = pltpu.make_async_remote_copy(
        src_ref=src,
        dst_ref=dst,
        send_sem=sems[0].at[at],
        recv_sem=sems[1].at[at],
        device_id=device,
        device_id_type=MESH,
    )
    copy.start()
    return copy


def gather_kernel(
    rows, n_dp, n_tensor, q, k, v, g, part, bias,
    qh, kh, vh, gh, logits_out, parts, logits,
    big_send, big_recv, local, halo_send, halo_recv, small_send, small_recv,
):
    dp, tensor, y, ring = place()
    width = 2 * HEAD
    after, before = lax.rem(dp + RING, n_dp), lax.rem(dp + n_dp - RING, n_dp)
    peers = [(ring_peer(dp, y, s), tensor) for s in range(1, RING)]
    mates = [(dp, lax.rem(tensor + s, n_tensor)) for s in range(1, n_tensor)]
    greet(peers + mates + [(after, tensor), (before, tensor)])

    small = (small_send, small_recv)
    outs = [
        send(part.at[pl.ds(pl.multiple_of(mate[1] * 8, 8), 8)], parts.at[s], small, s, mate)
        for s, mate in enumerate(mates)
    ]
    copies, own = {}, []
    for a, (src, dst, first) in enumerate(((k, kh, HALO), (v, vh, HALO), (q, qh, 0), (g, gh, 0))):
        at = pl.ds(pl.multiple_of(first + y * rows, rows), rows)
        for s in (2, 1, 3):
            peer = peers[s - 1]
            there = lax.rem(y + s, RING)
            cols = pl.ds(pl.multiple_of(there * width, width), width)
            copies[a, s] = send(src.at[:, cols], dst.at[at], (big_send, big_recv), a * 3 + s - 1, peer)
        mine = pltpu.make_async_copy(
            src.at[:, pl.ds(pl.multiple_of(y * width, width), width)], dst.at[at], local.at[a]
        )
        mine.start()
        own.append(mine)

    for copy in outs:
        copy.wait()
    total = part[pl.ds(pl.multiple_of(tensor * 8, 8), 8), :] + bias[:, :1]
    for s in range(n_tensor - 1):
        total = total + parts[s]
    logits[2 + y] = total
    outs = [
        send(logits.at[2 + y], logits.at[2 + y], small, 4 + s, peer) for s, peer in enumerate(peers)
    ]
    for copy in outs:
        copy.wait()
    ahead = send(logits.at[4:6], logits.at[0:2], small, 8, (after, tensor))

    for copy in own[:2]:
        copy.wait()
    for a in range(2):
        for s in range(1, RING):
            copies[a, s].wait()
    tail = pl.ds(RING * rows, HALO)
    halo = [
        send(ref.at[tail], ref.at[pl.ds(0, HALO)], (halo_send, halo_recv), a, (after, tensor))
        for a, ref in enumerate((kh, vh))
    ]
    for copy in own[2:]:
        copy.wait()
    for a in range(2, 4):
        for s in range(1, RING):
            copies[a, s].wait()
    ahead.wait()
    for copy in halo:
        copy.wait()
    logits_out[...] = logits[...]


def gather(n_dp, n_tensor, q, k, v, g, part, bias):
    rows = q.shape[0]
    home = RING * rows
    wide = jax.ShapeDtypeStruct((home, 2 * HEAD), BF16)
    long = jax.ShapeDtypeStruct((home + HALO, 2 * HEAD), BF16)
    dma = pltpu.SemaphoreType.DMA
    hbm, vmem = pl.BlockSpec(memory_space=pl.ANY), pl.BlockSpec(memory_space=pltpu.VMEM)
    return pl.pallas_call(
        functools.partial(gather_kernel, rows, n_dp, n_tensor),
        out_shape=(wide, long, long, wide, jax.ShapeDtypeStruct((6, 8, rows), F32)),
        in_specs=[hbm] * 4 + [vmem] * 2,
        out_specs=(hbm, hbm, hbm, hbm, vmem),
        scratch_shapes=[
            pltpu.VMEM((max(1, n_tensor - 1), 8, rows), F32),
            pltpu.VMEM((6, 8, rows), F32),
            dma((12,)), dma((12,)), dma((4,)), dma((2,)), dma((2,)), dma((9,)), dma((9,)),
        ],
        compiler_params=pltpu.CompilerParams(collective_id=0, has_side_effects=True),
        name="gather",
    )(q, k, v, g, part, bias)


def attend_kernel(
    q, k, v, g, decay, starts,
    dq, dk_own, dv_own, dk_halo, dv_halo, row_out, col_out,
    k_t, decay_col, score, grad, dk, dv, col,
):
    scale = HEAD ** (-0.5)
    window = k.shape[0]
    home = q.shape[0]
    chunks = BAND // TILE
    nt = (((1,), (1,)), ((), ()))
    for c in range(window // 512):
        at = slice(c * 512, (c + 1) * 512)
        k_t[:, at] = k[at, :].T
        decay_col[at, :] = decay[0, :, at].T
    dk[...] = jnp.zeros_like(dk)
    dv[...] = jnp.zeros_like(dv)
    col[...] = jnp.zeros_like(col)
    key_at = lax.broadcasted_iota(jnp.int32, (TILE, TILE), 0)
    query_at = lax.broadcasted_iota(jnp.int32, (TILE, TILE), 1)

    def fold(x, combine):
        out = x[:8]
        for r in range(8, x.shape[0], 8):
            out = combine(out, x[r : r + 8])
        return out

    def tile(t, carry):
        base = pl.multiple_of(t * TILE, TILE)
        mine = pl.ds(base, TILE)
        q_t, g_t = q[mine, :], g[mine, :]
        first = starts[0:1, mine] - base
        top = jnp.full((8, TILE), DEAD, F32)
        for c in range(chunks):
            at = pl.ds(base + c * TILE, TILE)
            s = lax.dot_general(k[at, :], q_t, nt, preferred_element_type=F32)
            s = s * (scale * LOG2E) - decay_col[at, 0:1]
            live = key_at >= first - c * TILE
            if c == chunks - 1:
                live = live & (key_at <= query_at)
            s = jnp.where(live, s, DEAD)
            score[c] = s
            top = jnp.maximum(top, fold(s, jnp.maximum))
        top = jnp.max(top, axis=0, keepdims=True)
        total = jnp.zeros((8, TILE), F32)
        delta = jnp.zeros((8, TILE), F32)
        for c in range(chunks):
            at = pl.ds(base + c * TILE, TILE)
            w = jnp.exp2(score[c] - top)
            d = lax.dot_general(v[at, :], g_t, nt, preferred_element_type=F32)
            score[c] = w
            grad[c] = d
            total = total + fold(w, jnp.add)
            delta = delta + fold(w * d, jnp.add)
        inverse = 1.0 / jnp.sum(total, axis=0, keepdims=True)
        delta = jnp.sum(delta, axis=0, keepdims=True) * inverse
        dq_t = jnp.zeros((HEAD, TILE), F32)
        row = jnp.zeros((8, TILE), F32)
        for c in range(chunks):
            at = pl.ds(base + c * TILE, TILE)
            p = score[c] * inverse
            ds = p * (grad[c] - delta)
            low = ds.astype(BF16)
            row = row + fold(ds, jnp.add)
            col[at, :] += ds[:, :HEAD] + ds[:, HEAD:]
            dv[at, :] += jnp.dot(p.astype(BF16), g_t, preferred_element_type=F32)
            dk[at, :] += jnp.dot(low, q_t, preferred_element_type=F32)
            dq_t = dq_t + jnp.dot(k_t[:, at], low, preferred_element_type=F32)
        dq[mine, :] = (dq_t * scale).T.astype(BF16)
        row_out[0, :, mine] = jnp.broadcast_to(jnp.sum(row, axis=0, keepdims=True), (8, TILE))
        return carry

    lax.fori_loop(0, home // TILE, tile, 0)
    dk_halo[...] = (dk[:HALO, :] * scale).astype(BF16)
    dv_halo[...] = dv[:HALO, :].astype(BF16)
    dk_own[...] = dk[HALO:, :] * scale
    dv_own[...] = dv[HALO:, :]
    ones = jnp.ones((8, HEAD), F32)
    col_out[0] = lax.dot_general(
        ones, col[...], nt, precision=lax.Precision.HIGHEST, preferred_element_type=F32
    )


def attend(qh, kh, vh, gh, decay, starts):
    home, window = qh.shape[0], kh.shape[0]
    chunks = BAND // TILE

    def cols(rows):
        return pl.BlockSpec((rows, HEAD), lambda h: (0, h))

    def flat(size):
        return pl.BlockSpec((1, 8, size), lambda h: (h, 0, 0))

    def shape(rows, dtype):
        return jax.ShapeDtypeStruct((rows, 2 * HEAD), dtype)

    return pl.pallas_call(
        attend_kernel,
        grid=(2,),
        out_shape=(
            shape(home, BF16),
            shape(home, F32),
            shape(home, F32),
            shape(HALO, BF16),
            shape(HALO, BF16),
            jax.ShapeDtypeStruct((2, 8, home), F32),
            jax.ShapeDtypeStruct((2, 8, window), F32),
        ),
        in_specs=[
            cols(home), cols(window), cols(window), cols(home), flat(window),
            pl.BlockSpec((8, home), lambda h: (0, 0)),
        ],
        out_specs=(cols(home), cols(home), cols(home), cols(HALO), cols(HALO), flat(home), flat(window)),
        scratch_shapes=[
            pltpu.VMEM((HEAD, window), BF16),
            pltpu.VMEM((window, 8), F32),
            pltpu.VMEM((chunks, TILE, TILE), F32),
            pltpu.VMEM((chunks, TILE, TILE), F32),
            pltpu.VMEM((window, HEAD), F32),
            pltpu.VMEM((window, HEAD), F32),
            pltpu.VMEM((window, HEAD), F32),
        ],
        compiler_params=pltpu.CompilerParams(vmem_limit_bytes=48 * 2**20),
        name="attend",
    )(qh, kh, vh, gh, decay, starts)


def scatter_kernel(
    rows, n_dp, dq, dk_own, dv_own, dk_halo, dv_halo, cols,
    dq_out, dk_out, dv_out, cols_out,
    halo, low, cols_in, big_send, big_recv, local, halo_send, halo_recv,
):
    dp, tensor, y, ring = place()
    width = 2 * HEAD
    home = RING * rows
    after, before = lax.rem(dp + RING, n_dp), lax.rem(dp + n_dp - RING, n_dp)
    peers = [(ring_peer(dp, y, s), tensor) for s in range(1, RING)]
    greet(peers + [(after, tensor), (before, tensor)])
    sems = (halo_send, halo_recv)
    back = [
        send(cols, cols_in, sems, 2, (before, tensor)),
        send(dk_halo, halo.at[0], sems, 0, (before, tensor)),
        send(dv_halo, halo.at[1], sems, 1, (before, tensor)),
    ]
    mine = pl.ds(pl.multiple_of(y * rows, rows), rows)
    here = pl.ds(pl.multiple_of(y * width, width), width)
    waits = []

    def spread(src, dst, a):
        for s in (2, 1, 3):
            there = lax.rem(y + s, RING)
            at = pl.ds(pl.multiple_of(there * rows, rows), rows)
            waits.append(send(src.at[at], dst.at[:, here], (big_send, big_recv), a * 3 + s - 1, peers[s - 1]))
        copy = pltpu.make_async_copy(src.at[mine], dst.at[:, here], local.at[a])
        copy.start()
        waits.append(copy)

    spread(dq, dq_out, 0)
    split = home - HALO
    for a, own in enumerate((dk_own, dv_own)):
        low[a, :split, :] = own[:split, :].astype(BF16)
    for a, (own, out) in enumerate(((dk_own, dk_out), (dv_own, dv_out))):
        back[a + 1].wait()
        low[a, split:, :] = (own[split:, :] + halo[a].astype(F32)).astype(BF16)
        spread(low.at[a], out, a + 1)
    back[0].wait()
    cols_out[...] = cols_in[...]
    for copy in waits:
        copy.wait()


def scatter(n_dp, dq, dk_own, dv_own, dk_halo, dv_halo, cols):
    home = dq.shape[0]
    rows = home // RING
    out = jax.ShapeDtypeStruct((rows, 8 * HEAD), BF16)
    dma = pltpu.SemaphoreType.DMA
    hbm, vmem = pl.BlockSpec(memory_space=pl.ANY), pl.BlockSpec(memory_space=pltpu.VMEM)
    return pl.pallas_call(
        functools.partial(scatter_kernel, rows, n_dp),
        out_shape=(out, out, out, jax.ShapeDtypeStruct(cols.shape, F32)),
        in_specs=[hbm, vmem, vmem, hbm, hbm, vmem],
        out_specs=(hbm, hbm, hbm, vmem),
        scratch_shapes=[
            pltpu.VMEM((2, HALO, 2 * HEAD), BF16),
            pltpu.VMEM((2, home, 2 * HEAD), BF16),
            pltpu.VMEM(cols.shape, F32),
            dma((9,)), dma((9,)), dma((3,)), dma((3,)), dma((3,)),
        ],
        compiler_params=pltpu.CompilerParams(
            collective_id=1, has_side_effects=True, vmem_limit_bytes=48 * 2**20
        ),
        name="scatter",
    )(dq, dk_own, dv_own, dk_halo, dv_halo, cols)


def tail_kernel(
    nz, nx, n_tensor, gate, x, bias,
    weight_out, bias_out,
    gates, wide, term, first, second, third, b_first, b_second, b_third, total, gathered,
    g_send, g_recv, t_send, t_recv, y_send, y_recv, z_send, z_recv, x_send, x_recv, w_send, w_recv, v_send, v_recv,
):
    dp, tensor, y, ring = place()
    part = nz * RING
    xh = dp // part
    z = lax.rem(dp, part) // RING
    peers = [(ring_peer(dp, y, s), tensor) for s in range(1, RING)]
    mates = [(dp, lax.rem(tensor + s, n_tensor)) for s in range(1, n_tensor)]
    line = [(xh * part + lax.rem(z + s, nz) * RING + y, tensor) for s in range(1, nz)]
    cross = [(lax.rem(xh + s, nx) * part + z * RING + y, tensor) for s in range(1, nx)]
    greet(peers + mates + line + cross)

    copies = [
        send(gate.at[lax.rem(y + s + 1, RING)], gates.at[s], (g_send, g_recv), s, peer)
        for s, peer in enumerate(peers)
    ]
    copies_b = [send(bias, b_first.at[s], (g_send, g_recv), 3 + s, peer) for s, peer in enumerate(peers)]
    mine = gate[y]
    for s, copy in enumerate(copies):
        copy.wait()
        mine = mine + gates[s]
    rows = pl.ds(pl.multiple_of(tensor * 8, 8), 8)
    wide[rows, :] = mine
    copies = [
        send(wide.at[rows], wide.at[rows], (t_send, t_recv), s, mate) for s, mate in enumerate(mates)
    ]
    b_sum = bias[...]
    for s, copy in enumerate(copies_b):
        copy.wait()
        b_sum = b_sum + b_first[s]
    total[1] = b_sum
    for copy in copies:
        copy.wait()
    term[...] = jnp.dot(wide[...].astype(BF16), x[...], preferred_element_type=F32)

    block = term.shape[0] // RING
    copies = [
        send(
            term.at[pl.ds(pl.multiple_of(lax.rem(y + s + 1, RING) * block, block), block)],
            first.at[s], (y_send, y_recv), s, peer,
        )
        for s, peer in enumerate(peers)
    ]
    here = pl.ds(pl.multiple_of(y * block, block), block)
    part_sum = term[here, :]
    for s, copy in enumerate(copies):
        copy.wait()
        part_sum = part_sum + first[s]
    term[here, :] = part_sum

    wd = term.shape[1] // nz

    def lanes(at):
        return pl.ds(pl.multiple_of(at * wd, wd), wd)

    copies = [
        send(term.at[here, lanes(lax.rem(z + s + 1, nz))], second.at[s], (z_send, z_recv), s, device)
        for s, device in enumerate(line)
    ]
    copies_b = [
        send(total.at[1], b_second.at[s], (z_send, z_recv), nz - 1 + s, device)
        for s, device in enumerate(line)
    ]
    piece = term[here, lanes(z)]
    for s, copy in enumerate(copies):
        copy.wait()
        piece = piece + second[s]
    for s, copy in enumerate(copies_b):
        copy.wait()
        b_sum = b_sum + b_second[s]
    total[0, :, :wd] = piece
    total[1] = b_sum
    copies = [
        send(total, third.at[s], (x_send, x_recv), s, device) for s, device in enumerate(cross)
    ]
    for s, copy in enumerate(copies):
        copy.wait()
        piece = piece + third[s, 0, :, :wd]
        b_sum = b_sum + third[s, 1]
    bias_out[...] = b_sum

    gathered[here, lanes(z)] = piece
    copies = [
        send(gathered.at[here, lanes(z)], gathered.at[here, lanes(z)], (w_send, w_recv), s, device)
        for s, device in enumerate(line)
    ]
    for copy in copies:
        copy.wait()
    copies = [
        send(gathered.at[here], gathered.at[here], (v_send, v_recv), s, peer)
        for s, peer in enumerate(peers)
    ]
    for copy in copies:
        copy.wait()
    weight_out[...] = gathered[...]


def tail(nz, nx, n_tensor, gate, x, bias):
    heads, width = 8 * n_tensor, x.shape[1]
    rows = gate.shape[2]
    wd = width // nz
    pad = max(wd, 128)
    assert pad == 128 or nz < 8
    block = heads // RING
    dma = pltpu.SemaphoreType.DMA
    vmem = pl.BlockSpec(memory_space=pltpu.VMEM)
    return pl.pallas_call(
        functools.partial(tail_kernel, nz, nx, n_tensor),
        out_shape=(jax.ShapeDtypeStruct((heads, width), F32), jax.ShapeDtypeStruct((8, pad), F32)),
        in_specs=[vmem] * 3,
        out_specs=(vmem, vmem),
        scratch_shapes=[
            pltpu.VMEM((3, 8, rows), F32),
            pltpu.VMEM((heads, rows), F32),
            pltpu.VMEM((heads, width), F32),
            pltpu.VMEM((3, block, width), F32),
            pltpu.VMEM((max(1, nz - 1), block, wd), F32),
            pltpu.VMEM((max(1, nx - 1), 2, 8, pad), F32),
            pltpu.VMEM((3, 8, pad), F32),
            pltpu.VMEM((max(1, nz - 1), 8, pad), F32),
            pltpu.VMEM((1, 8, pad), F32),
            pltpu.VMEM((2, 8, pad), F32),
            pltpu.VMEM((heads, width), F32),
            dma((6,)), dma((6,)), dma((3,)), dma((3,)), dma((3,)), dma((3,)),
            dma((14,)), dma((14,)), dma((1,)), dma((1,)), dma((7,)), dma((7,)), dma((3,)), dma((3,)),
        ],
        compiler_params=pltpu.CompilerParams(collective_id=2, has_side_effects=True),
        name="tail",
    )(gate, x, bias)


def shards(n_dp, n_tensor, q, k, v, g, x, gate_weight, gate_bias, doc_lengths):
    rows = q.shape[0]
    home, window = RING * rows, RING * rows + HALO
    dp, tensor, y, ring = place()
    part = lax.dot_general(gate_weight, x, (((0,), (1,)), ((), ())), preferred_element_type=F32)
    bias = jnp.broadcast_to(gate_bias[:, None], (8, 128))
    qh, kh, vh, gh, logits = gather(n_dp, n_tensor, q, k, v, g, part, bias)

    doc_ends = jnp.cumsum(doc_lengths)
    origin = ring * rows - HALO
    positions = ring * rows + jnp.arange(home, dtype=jnp.int32)
    passed = positions[None, :] >= doc_ends[:, None]
    starts = jnp.max(jnp.where(passed, doc_ends[:, None], 0), axis=0) - origin
    logit = lax.dynamic_slice_in_dim(logits, 2 * y, 2, 1).transpose(1, 0, 2).reshape(2, window)
    decay = jnp.cumsum(jax.nn.log_sigmoid(logit), axis=1) * LOG2E
    decay = jnp.broadcast_to(decay[:, None, :], (2, 8, window))
    dq, dk_own, dv_own, dk_halo, dv_halo, row_sum, col_sum = attend(
        qh, kh, vh, gh, decay, jnp.broadcast_to(starts[None, :], (8, home))
    )

    row_sum, col_sum = row_sum[:, 0], col_sum[:, 0]
    decay_grad = row_sum - col_sum[:, HALO:]
    crossing = jnp.sum(jnp.where(starts[None, :] < HALO, decay_grad, 0.0), axis=1)
    cols = jnp.concatenate([col_sum[:, :HALO], jnp.broadcast_to(crossing[:, None], (2, 128))], axis=1)
    cols = jnp.concatenate([cols, jnp.zeros((6, HALO + 128), F32)])
    query_grad, key_grad, value_grad, cols = scatter(n_dp, dq, dk_own, dv_own, dk_halo, dv_halo, cols)

    decay_grad = decay_grad - jnp.pad(cols[:2, :HALO], ((0, 0), (home - HALO, 0)))
    keep_grad = jnp.flip(jnp.cumsum(jnp.flip(decay_grad, 1), axis=1), 1) + cols[:2, HALO : HALO + 1]
    gate_grad = keep_grad * jax.nn.sigmoid(-logit[:, HALO:])
    low = gate_grad.astype(BF16).astype(F32).reshape(2, RING, rows).transpose(1, 0, 2)
    gate = lax.dynamic_update_slice(jnp.zeros((RING, 8, rows), F32), low, (0, 2 * y, 0))
    nx = 2
    nz = n_dp // (RING * nx)
    pad = max(x.shape[1] // nz, 128)
    sums = jnp.broadcast_to(jnp.sum(gate_grad, axis=1)[:, None], (2, pad))
    sums = lax.dynamic_update_slice(jnp.zeros((8, pad), F32), sums, (2 * y, 0))
    weight, sums = tail(nz, nx, n_tensor, gate, x, sums)
    return query_grad, key_grad, value_grad, weight.T, sums[:, 0]


def solution(mesh):
    return jax.shard_map(
        functools.partial(shards, mesh.shape["dp"], mesh.shape["tensor"]),
        mesh=mesh,
        in_specs=(
            P("dp", "tensor"),
            P("dp", "tensor"),
            P("dp", "tensor"),
            P("dp", "tensor"),
            P("dp", "tensor"),
            P("tensor", None),
            P("tensor"),
            P(),
        ),
        out_specs=(
            P("dp", "tensor"),
            P("dp", "tensor"),
            P("dp", "tensor"),
            P("tensor", None),
            P("tensor"),
        ),
        check_vma=False,
    )
```

```python
import functools
import math

import jax
import jax.numpy as jnp
from jax import lax
from jax.experimental import pallas as pl
from jax.experimental.pallas import tpu as pltpu
from jax.sharding import PartitionSpec as P

RING = 4
HALO = 1024
HEAD = 128
TILE = 256
BAND = HALO + TILE
LOG2E = math.log2(math.e)
DEAD = -1e30
MESH = pl.DeviceIdType.MESH
F32 = jnp.float32
BF16 = jnp.bfloat16


def place():
    dp, tensor = lax.axis_index("dp"), lax.axis_index("tensor")
    y = lax.rem(dp, RING)
    return dp, tensor, y, dp - y


def ring_peer(dp, y, step):
    return dp - y + lax.rem(y + step, RING)


def greet(devices):
    barrier = pltpu.get_barrier_semaphore()
    for device in devices:
        pl.semaphore_signal(barrier, inc=1, device_id=device, device_id_type=MESH)
    pl.semaphore_wait(barrier, len(devices))


def send(src, dst, sems, at, device):
    copy = pltpu.make_async_remote_copy(
        src_ref=src,
        dst_ref=dst,
        send_sem=sems[0].at[at],
        recv_sem=sems[1].at[at],
        device_id=device,
        device_id_type=MESH,
    )
    copy.start()
    return copy


def fold(x, combine):
    out = x[:8]
    for r in range(8, x.shape[0], 8):
        out = combine(out, x[r : r + 8])
    return out


def running(chunks, later):
    a = lax.broadcasted_iota(jnp.int32, (128, 128), 0)
    b = lax.broadcasted_iota(jnp.int32, (128, 128), 1)
    ones = jnp.where(a >= b if later else a <= b, 1.0, 0.0).astype(F32)
    sums = jnp.dot(
        jnp.concatenate(chunks), ones, precision=lax.Precision.HIGHEST, preferred_element_type=F32
    )
    return [sums[8 * i : 8 * i + 8] for i in range(len(chunks))]


def tile_step(scale, q, k, v, g, k_t, decay_col, starts, score, grad, dk, dv, col, dq, rows_sum, t):
    chunks = BAND // TILE
    nt = (((1,), (1,)), ((), ()))
    base = pl.multiple_of(t * TILE, TILE)
    mine = pl.ds(base, TILE)
    q_t, g_t = q[mine, :], g[mine, :]
    first = starts[0:1, mine] - base
    key_at = lax.broadcasted_iota(jnp.int32, (TILE, TILE), 0)
    top = jnp.full((8, TILE), DEAD, F32)
    for c in range(chunks):
        at = pl.ds(base + c * TILE, TILE)
        s = lax.dot_general(k[at, :], q_t, nt, preferred_element_type=F32)
        s = s * (scale * LOG2E) - decay_col[at, 0:1]
        live = key_at >= first - c * TILE
        if c == chunks - 1:
            live = live & (key_at <= lax.broadcasted_iota(jnp.int32, (TILE, TILE), 1))
        s = jnp.where(live, s, DEAD)
        score[c] = s
        top = jnp.maximum(top, fold(s, jnp.maximum))
    top = jnp.max(top, axis=0, keepdims=True)
    total = jnp.zeros((8, TILE), F32)
    delta = jnp.zeros((8, TILE), F32)
    for c in range(chunks):
        at = pl.ds(base + c * TILE, TILE)
        w = jnp.exp2(score[c] - top)
        d = lax.dot_general(v[at, :], g_t, nt, preferred_element_type=F32)
        score[c] = w
        grad[c] = d
        total = total + fold(w, jnp.add)
        delta = delta + fold(w * d, jnp.add)
    inverse = 1.0 / jnp.sum(total, axis=0, keepdims=True)
    delta = jnp.sum(delta, axis=0, keepdims=True) * inverse
    dq_t = jnp.zeros((HEAD, TILE), F32)
    row = jnp.zeros((8, TILE), F32)
    for c in range(chunks):
        at = pl.ds(base + c * TILE, TILE)
        p = score[c] * inverse
        ds = p * (grad[c] - delta)
        low = ds.astype(BF16)
        row = row + fold(ds, jnp.add)
        col[at, :] += ds[:, :HEAD] + ds[:, HEAD:]
        dv[at, :] += jnp.dot(p.astype(BF16), g_t, preferred_element_type=F32)
        dk[at, :] += jnp.dot(low, q_t, preferred_element_type=F32)
        dq_t = dq_t + jnp.dot(k_t[:, at], low, preferred_element_type=F32)
    dq[mine, :] = (dq_t * scale).T.astype(BF16)
    rows_sum[:, mine] = jnp.broadcast_to(jnp.sum(row, axis=0, keepdims=True), (8, TILE))


def main_kernel(
    rows, n_dp, n_tensor, nz, nx,
    q, k, v, g, x, gate_weight, gate_bias, lengths,
    dq_out, dk_out, dv_out, weight_out, bias_out,
    qh, kh, vh, gh, parts, part, logits, decay, starts,
    k_t, decay_col, score, grad, dk, dv, col, dq, row_sum, col_sum,
    halo_out, halo_in, low, cols_out, cols_in,
    gate, gates, wide, term, first, second, third, b_first, b_second, b_third, total, gathered,
    in_send, in_recv, own_in, relay_send, relay_recv, small_send, small_recv,
    out_send, out_recv, own_out, halo_send, halo_recv,
    g_send, g_recv, t_send, t_recv, y_send, y_recv, z_send, z_recv, x_send, x_recv, w_send, w_recv, v_send, v_recv,
):
    scale = HEAD ** (-0.5)
    home, window = RING * rows, RING * rows + HALO
    dp, tensor, y, ring = place()
    after, before = lax.rem(dp + RING, n_dp), lax.rem(dp + n_dp - RING, n_dp)
    plane = nz * RING
    xh = dp // plane
    z = lax.rem(dp, plane) // RING
    peers = [(ring_peer(dp, y, s), tensor) for s in range(1, RING)]
    mates = [(dp, lax.rem(tensor + s, n_tensor)) for s in range(1, n_tensor)]
    line = [(xh * plane + lax.rem(z + s, nz) * RING + y, tensor) for s in range(1, nz)]
    cross = [(lax.rem(xh + s, nx) * plane + z * RING + y, tensor) for s in range(1, nx)]
    greet(peers + mates + [(after, tensor), (before, tensor)] + line + cross)

    def columns(shard, h):
        return pl.ds(pl.multiple_of(shard * (2 * HEAD) + h * HEAD, HEAD), HEAD)

    def shard_rows(shard, offset=0):
        return pl.ds(pl.multiple_of(offset + shard * rows, rows), rows)

    arrive, own = {}, {}

    def fetch(h):
        for a, (src, dst, ahead) in enumerate(((k, kh, HALO), (v, vh, HALO), (q, qh, 0), (g, gh, 0))):
            at = shard_rows(y, ahead)
            for s in (2, 1, 3):
                arrive[h, a, s] = send(
                    src.at[:, columns(lax.rem(y + s, RING), h)], dst.at[h, at],
                    (in_send, in_recv), h * 12 + a * 3 + s - 1, peers[s - 1],
                )
            own[h, a] = pltpu.make_async_copy(
                src.at[:, columns(y, h)], dst.at[h, at], own_in.at[h * 4 + a]
            )
            own[h, a].start()

    def arrived(h, arrays):
        for a in arrays:
            own[h, a].wait()
            for s in range(1, RING):
                arrive[h, a, s].wait()

    def relay(h):
        tail = pl.ds(home, HALO)
        return [
            send(ref.at[h, tail], ref.at[h, pl.ds(0, HALO)], (relay_send, relay_recv), h * 2 + a, (after, tensor))
            for a, ref in enumerate((kh, vh))
        ]

    fetch(0)

    part[...] = jnp.dot(x[...], gate_weight[...], preferred_element_type=F32).T
    small = (small_send, small_recv)
    outs = [
        send(part.at[pl.ds(pl.multiple_of(mate[1] * 8, 8), 8)], parts.at[s], small, s, mate)
        for s, mate in enumerate(mates)
    ]
    docs = lengths.shape[1]
    at_0 = lax.broadcasted_iota(jnp.int32, (docs, docs), 0)
    at_1 = lax.broadcasted_iota(jnp.int32, (docs, docs), 1)
    ends = jnp.sum(
        jnp.where(at_1 <= at_0, jnp.broadcast_to(lengths[...], (docs, docs)).astype(F32), 0.0),
        axis=1, keepdims=True,
    ).astype(jnp.int32)
    origin = ring * rows - HALO
    for c in range(home // 512):
        position = ring * rows + c * 512 + lax.broadcasted_iota(jnp.int32, (docs, 512), 1)
        begun = fold(jnp.where(ends <= position, ends, 0), jnp.maximum)
        starts[:, c * 512 : (c + 1) * 512] = jnp.broadcast_to(
            jnp.max(begun, axis=0, keepdims=True) - origin, (8, 512)
        )
    eye = lax.broadcasted_iota(jnp.int32, (8, 8), 0) == lax.broadcasted_iota(jnp.int32, (8, 8), 1)
    bias = jnp.sum(
        jnp.where(eye, jnp.broadcast_to(gate_bias[...], (8, 8)), 0.0), axis=1, keepdims=True
    )
    for copy in outs:
        copy.wait()
    logit = part[pl.ds(pl.multiple_of(tensor * 8, 8), 8), :] + bias
    for s in range(n_tensor - 1):
        logit = logit + parts[s]
    logits[2 + y] = logit
    spread = [
        send(logits.at[2 + y], logits.at[2 + y], small, 3 + s, peer) for s, peer in enumerate(peers)
    ]
    arrived(0, (0, 1))
    relays = relay(0)
    fetch(1)
    for copy in spread:
        copy.wait()
    ahead = send(logits.at[4:6], logits.at[0:2], small, 6, (after, tensor))
    for h in range(2):
        dk[h] = jnp.zeros((window, HEAD), F32)
        dv[h] = jnp.zeros((window, HEAD), F32)
        col[h] = jnp.zeros((window, HEAD), F32)
    ahead.wait()
    pieces = []
    for s in range(6):
        keep = logits[s]
        keep = -(jnp.maximum(-keep, 0.0) + jnp.log1p(jnp.exp(-jnp.abs(keep))))
        pieces += [keep[:, c * 128 : (c + 1) * 128] * LOG2E for c in range(rows // 128)]
    carry = jnp.zeros((8, 1), F32)
    for i, piece in enumerate(running(pieces, False)):
        decay[:, i * 128 : (i + 1) * 128] = piece + carry
        carry = carry + piece[:, 127:128]
    which = lax.broadcasted_iota(jnp.int32, (8, 512), 0)

    def prepare(h, part_of):
        for c in part_of:
            at = slice(c * 512, (c + 1) * 512)
            k_t[:, at] = kh[h, at, :].T
            mine = jnp.where(which == 2 * y + h, decay[:, at], 0.0)
            decay_col[at, :] = jnp.broadcast_to(jnp.sum(mine, axis=0, keepdims=True), (8, 512)).T

    def tiles(h, low_tile, high_tile):
        def step(t, carry):
            tile_step(
                scale, qh.at[h], kh.at[h], vh.at[h], gh.at[h], k_t, decay_col, starts, score, grad,
                dk.at[h], dv.at[h], col.at[h], dq.at[h], row_sum.at[h], t,
            )
            return carry

        lax.fori_loop(low_tile, high_tile, step, 0)

    leave = []

    def give(src, dst, h, a):
        for s in (2, 1, 3):
            leave.append(send(
                src.at[shard_rows(lax.rem(y + s, RING))], dst.at[:, columns(y, h)],
                (out_send, out_recv), h * 9 + a * 3 + s - 1, peers[s - 1],
            ))
        copy = pltpu.make_async_copy(src.at[shard_rows(y)], dst.at[:, columns(y, h)], own_out.at[h * 3 + a])
        copy.start()
        leave.append(copy)

    back = {}

    def give_halo(h):
        halo_out[h, 0] = (dk[h, :HALO, :] * scale).astype(BF16)
        halo_out[h, 1] = dv[h, :HALO, :].astype(BF16)
        for a in range(2):
            back[h, a] = send(
                halo_out.at[h, a], halo_in.at[h, a], (halo_send, halo_recv), h * 2 + a, (before, tensor)
            )

    def give_rest(h):
        split = home - HALO
        for a, (grads, factor, out) in enumerate(((dk, scale, dk_out), (dv, 1.0, dv_out))):
            low[h, a, :split, :] = (grads[h, HALO:home, :] * factor).astype(BF16)
            back[h, a].wait()
            low[h, a, split:, :] = (
                grads[h, home:, :] * factor + halo_in[h, a].astype(F32)
            ).astype(BF16)
            give(low.at[h, a], out, h, a + 1)

    blocks = window // 512
    halo_blocks = HALO // 512
    half = HALO // TILE
    arrived(0, (2, 3))
    prepare(0, range(halo_blocks, blocks))
    tiles(0, half, home // TILE)
    arrived(1, (0, 1))
    relays_1 = relay(1)
    for copy in relays:
        copy.wait()
    prepare(0, range(halo_blocks))
    tiles(0, 0, half)
    give_halo(0)
    give(dq.at[0], dq_out, 0, 0)
    arrived(1, (2, 3))
    for copy in relays_1:
        copy.wait()
    prepare(1, range(blocks))
    tiles(1, 0, half)
    give_halo(1)
    give_rest(0)
    tiles(1, half, home // TILE)
    give(dq.at[1], dq_out, 1, 0)

    nt = (((1,), (1,)), ((), ()))
    ones = jnp.ones((8, HEAD), F32)
    crossed = starts[...] < HALO
    for h in range(2):
        col_sum[h] = lax.dot_general(
            ones, col[h], nt, precision=lax.Precision.HIGHEST, preferred_element_type=F32
        )
        cols_out[h, :, :HALO] = col_sum[h, :, :HALO]
        here = jnp.where(crossed, row_sum[h] - col_sum[h, :, HALO:], 0.0)
        cols_out[h, :, HALO:] = jnp.broadcast_to(jnp.sum(here, axis=1, keepdims=True), (8, 128))
    cols = send(cols_out, cols_in, small, 7, (before, tensor))
    give_rest(1)
    cols.wait()

    which = lax.broadcasted_iota(jnp.int32, (8, 128), 0)
    pieces = []
    for c in range(home // 128):
        at = slice(c * 128, (c + 1) * 128)
        mine = []
        for h in range(2):
            term_h = row_sum[h, :, at] - col_sum[h, :, HALO + c * 128 : HALO + (c + 1) * 128]
            if c >= (home - HALO) // 128:
                off = c * 128 - (home - HALO)
                term_h = term_h - cols_in[h, :, off : off + 128]
            mine.append(term_h)
        pieces.append(jnp.where(which == 2 * y, mine[0], jnp.where(which == 2 * y + 1, mine[1], 0.0)))
    carry = jnp.where(
        which == 2 * y, cols_in[0, :, HALO:], jnp.where(which == 2 * y + 1, cols_in[1, :, HALO:], 0.0)
    )
    bias_sum = jnp.zeros((8, 1), F32)
    sums = running(pieces, True)
    for c in reversed(range(home // 128)):
        shard, off = divmod(c * 128, rows)
        keep = sums[c] + carry
        carry = carry + sums[c][:, 0:1]
        raw = logits[2 + shard, :, off : off + 128]
        down = jnp.exp(-jnp.abs(raw))
        gate_grad = keep * (jnp.where(raw >= 0, down, 1.0) / (1.0 + down))
        bias_sum = bias_sum + jnp.sum(gate_grad, axis=1, keepdims=True)
        gate[shard, :, off : off + 128] = gate_grad.astype(BF16).astype(F32)
    bias_mine = b_third.at[0]
    bias_mine[...] = jnp.broadcast_to(bias_sum, (8, 128))

    copies = [
        send(gate.at[lax.rem(y + s + 1, RING)], gates.at[s], (g_send, g_recv), s, peer)
        for s, peer in enumerate(peers)
    ]
    copies_b = [
        send(bias_mine, b_first.at[s], (g_send, g_recv), 3 + s, peer) for s, peer in enumerate(peers)
    ]
    mine = gate[y]
    for s, copy in enumerate(copies):
        copy.wait()
        mine = mine + gates[s]
    wide_at = pl.ds(pl.multiple_of(tensor * 8, 8), 8)
    wide[wide_at, :] = mine
    copies = [
        send(wide.at[wide_at], wide.at[wide_at], (t_send, t_recv), s, mate) for s, mate in enumerate(mates)
    ]
    b_sum = bias_mine[...]
    for s, copy in enumerate(copies_b):
        copy.wait()
        b_sum = b_sum + b_first[s]
    total[1] = b_sum
    for copy in copies:
        copy.wait()
    term[...] = jnp.dot(wide[...].astype(BF16), x[...], preferred_element_type=F32)

    block = term.shape[0] // RING
    copies = [
        send(
            term.at[pl.ds(pl.multiple_of(lax.rem(y + s + 1, RING) * block, block), block)],
            first.at[s], (y_send, y_recv), s, peer,
        )
        for s, peer in enumerate(peers)
    ]
    here = pl.ds(pl.multiple_of(y * block, block), block)
    part_sum = term[here, :]
    for s, copy in enumerate(copies):
        copy.wait()
        part_sum = part_sum + first[s]
    term[here, :] = part_sum

    wd = term.shape[1] // nz

    def lanes(at):
        return pl.ds(pl.multiple_of(at * wd, wd), wd)

    copies = [
        send(term.at[here, lanes(lax.rem(z + s + 1, nz))], second.at[s], (z_send, z_recv), s, device)
        for s, device in enumerate(line)
    ]
    copies_b = [
        send(total.at[1], b_second.at[s], (z_send, z_recv), nz - 1 + s, device)
        for s, device in enumerate(line)
    ]
    piece = term[here, lanes(z)]
    for s, copy in enumerate(copies):
        copy.wait()
        piece = piece + second[s]
    for s, copy in enumerate(copies_b):
        copy.wait()
        b_sum = b_sum + b_second[s]
    total[0] = piece
    total[1] = b_sum
    copies = [
        send(total, third.at[s], (x_send, x_recv), s, device) for s, device in enumerate(cross)
    ]
    for s, copy in enumerate(copies):
        copy.wait()
        piece = piece + third[s, 0]
        b_sum = b_sum + third[s, 1]
    bias_out[...] = b_sum

    gathered[here, lanes(z)] = piece
    copies = [
        send(gathered.at[here, lanes(z)], gathered.at[here, lanes(z)], (w_send, w_recv), s, device)
        for s, device in enumerate(line)
    ]
    for copy in copies:
        copy.wait()
    copies = [
        send(gathered.at[here], gathered.at[here], (v_send, v_recv), s, peer)
        for s, peer in enumerate(peers)
    ]
    for copy in copies:
        copy.wait()
    weight_out[...] = gathered[...]
    for copy in leave:
        copy.wait()


def shards(n_dp, n_tensor, q, k, v, g, x, gate_weight, gate_bias, doc_lengths):
    rows, width = q.shape
    home, window = RING * rows, RING * rows + HALO
    heads = 8 * n_tensor
    nx = 2
    nz = n_dp // (RING * nx)
    block = heads // RING
    assert width == 128 * nz and block == 8
    chunks = BAND // TILE
    hbm, vmem = pl.BlockSpec(memory_space=pl.ANY), pl.BlockSpec(memory_space=pltpu.VMEM)

    def dma(*sizes):
        return [pltpu.SemaphoreType.DMA((size,)) for size in sizes]

    out = jax.ShapeDtypeStruct((rows, width), BF16)
    pair = [pltpu.VMEM((2, window, HEAD), F32)]
    dq, dk, dv, weight, bias = pl.pallas_call(
        functools.partial(main_kernel, rows, n_dp, n_tensor, nz, nx),
        out_shape=(
            out, out, out,
            jax.ShapeDtypeStruct((heads, width), F32),
            jax.ShapeDtypeStruct((8, 128), F32),
        ),
        in_specs=[hbm] * 4 + [vmem] * 4,
        out_specs=(hbm, hbm, hbm, vmem, vmem),
        scratch_shapes=[
            pltpu.VMEM((2, home, HEAD), BF16),
            pltpu.VMEM((2, window, HEAD), BF16),
            pltpu.VMEM((2, window, HEAD), BF16),
            pltpu.VMEM((2, home, HEAD), BF16),
            pltpu.VMEM((n_tensor - 1, 8, rows), F32),
            pltpu.VMEM((heads, rows), F32),
            pltpu.VMEM((6, 8, rows), F32),
            pltpu.VMEM((8, window), F32),
            pltpu.VMEM((8, home), jnp.int32),
            pltpu.VMEM((HEAD, window), BF16),
            pltpu.VMEM((window, 8), F32),
            pltpu.VMEM((chunks, TILE, TILE), F32),
            pltpu.VMEM((chunks, TILE, TILE), F32),
            *(pair * 3),
            pltpu.VMEM((2, home, HEAD), BF16),
            pltpu.VMEM((2, 8, home), F32),
            pltpu.VMEM((2, 8, window), F32),
            pltpu.VMEM((2, 2, HALO, HEAD), BF16),
            pltpu.VMEM((2, 2, HALO, HEAD), BF16),
            pltpu.VMEM((2, 2, home, HEAD), BF16),
            pltpu.VMEM((2, 8, HALO + 128), F32),
            pltpu.VMEM((2, 8, HALO + 128), F32),
            pltpu.VMEM((RING, 8, rows), F32),
            pltpu.VMEM((3, 8, rows), F32),
            pltpu.VMEM((heads, rows), F32),
            pltpu.VMEM((heads, width), F32),
            pltpu.VMEM((3, block, width), F32),
            pltpu.VMEM((nz - 1, block, 128), F32),
            pltpu.VMEM((nx - 1, 2, 8, 128), F32),
            pltpu.VMEM((3, 8, 128), F32),
            pltpu.VMEM((nz - 1, 8, 128), F32),
            pltpu.VMEM((1, 8, 128), F32),
            pltpu.VMEM((2, 8, 128), F32),
            pltpu.VMEM((heads, width), F32),
            *dma(24, 24, 8, 4, 4, 8, 8),
            *dma(18, 18, 6, 4, 4),
            *dma(6, 6, 3, 3, 3, 3, 2 * (nz - 1), 2 * (nz - 1), 1, 1, nz - 1, nz - 1, 3, 3),
        ],
        compiler_params=pltpu.CompilerParams(
            collective_id=0, has_side_effects=True, vmem_limit_bytes=56 * 2**20
        ),
        name="main",
    )(q, k, v, g, x, gate_weight, gate_bias.reshape(1, 8), doc_lengths.reshape(1, -1))
    return dq, dk, dv, weight.T, bias[:, 0]


def solution(mesh):
    return jax.shard_map(
        functools.partial(shards, mesh.shape["dp"], mesh.shape["tensor"]),
        mesh=mesh,
        in_specs=(
            P("dp", "tensor"),
            P("dp", "tensor"),
            P("dp", "tensor"),
            P("dp", "tensor"),
            P("dp", "tensor"),
            P("tensor", None),
            P("tensor"),
            P(),
        ),
        out_specs=(
            P("dp", "tensor"),
            P("dp", "tensor"),
            P("dp", "tensor"),
            P("tensor", None),
            P("tensor"),
        ),
        check_vma=False,
    )
```

```python
import functools
import math

import jax
import jax.numpy as jnp
from jax import lax
from jax.experimental import pallas as pl
from jax.experimental.pallas import tpu as pltpu
from jax.sharding import PartitionSpec as P

RING = 4
HALO = 1024
HEAD = 128
TILE = 256
BAND = HALO + TILE
LOG2E = math.log2(math.e)
DEAD = -1e30
MESH = pl.DeviceIdType.MESH
F32 = jnp.float32
BF16 = jnp.bfloat16


def place():
    dp, tensor = lax.axis_index("dp"), lax.axis_index("tensor")
    y = lax.rem(dp, RING)
    return dp, tensor, y, dp - y


def ring_peer(dp, y, step):
    return dp - y + lax.rem(y + step, RING)


def greet(devices, meanwhile):
    barrier = pltpu.get_barrier_semaphore()
    for device in devices:
        pl.semaphore_signal(barrier, inc=1, device_id=device, device_id_type=MESH)
    meanwhile()
    pl.semaphore_wait(barrier, len(devices))


def send(src, dst, sems, at, device):
    copy = pltpu.make_async_remote_copy(
        src_ref=src,
        dst_ref=dst,
        send_sem=sems[0].at[at],
        recv_sem=sems[1].at[at],
        device_id=device,
        device_id_type=MESH,
    )
    copy.start()
    return copy


def fold(x, combine):
    out = x[:8]
    for r in range(8, x.shape[0], 8):
        out = combine(out, x[r : r + 8])
    return out


def running(chunks, later):
    a = lax.broadcasted_iota(jnp.int32, (128, 128), 0)
    b = lax.broadcasted_iota(jnp.int32, (128, 128), 1)
    ones = jnp.where(a >= b if later else a <= b, 1.0, 0.0).astype(F32)
    sums = jnp.dot(
        jnp.concatenate(chunks), ones, precision=lax.Precision.HIGHEST, preferred_element_type=F32
    )
    return [sums[8 * i : 8 * i + 8] for i in range(len(chunks))]


def tile_step(scale, q, k, v, g, k_t, decay_col, starts, score, grad, dk, dv, col, dq, rows_sum, t):
    chunks = BAND // TILE
    nt = (((1,), (1,)), ((), ()))
    base = pl.multiple_of(t * TILE, TILE)
    mine = pl.ds(base, TILE)
    q_t, g_t = q[mine, :], g[mine, :]
    first = starts[0:1, mine] - base
    key_at = lax.broadcasted_iota(jnp.int32, (TILE, TILE), 0)
    top = jnp.full((8, TILE), DEAD, F32)
    for c in range(chunks):
        at = pl.ds(base + c * TILE, TILE)
        s = lax.dot_general(k[at, :], q_t, nt, preferred_element_type=F32)
        s = s * (scale * LOG2E) - decay_col[at, 0:1]
        live = key_at >= first - c * TILE
        if c == chunks - 1:
            live = live & (key_at <= lax.broadcasted_iota(jnp.int32, (TILE, TILE), 1))
        s = jnp.where(live, s, DEAD)
        score[c] = s
        top = jnp.maximum(top, fold(s, jnp.maximum))
    top = jnp.max(top, axis=0, keepdims=True)
    total = jnp.zeros((8, TILE), F32)
    delta = jnp.zeros((8, TILE), F32)
    for c in range(chunks):
        at = pl.ds(base + c * TILE, TILE)
        w = jnp.exp2(score[c] - top)
        d = lax.dot_general(v[at, :], g_t, nt, preferred_element_type=F32)
        score[c] = w
        grad[c] = d
        total = total + fold(w, jnp.add)
        delta = delta + fold(w * d, jnp.add)
    total = jnp.sum(total, axis=0, keepdims=True)
    inverse = 1.0 / total
    delta = jnp.sum(delta, axis=0, keepdims=True) * inverse
    rows_sum[:, mine] = jnp.broadcast_to(delta - delta * (total * inverse), (8, TILE))
    dq_t = jnp.zeros((HEAD, TILE), F32)
    for c in range(chunks):
        at = pl.ds(base + c * TILE, TILE)
        p = score[c] * inverse
        ds = p * (grad[c] - delta)
        low = ds.astype(BF16)
        col[at, :] += ds[:, :HEAD] + ds[:, HEAD:]
        dv[at, :] += jnp.dot(p.astype(BF16), g_t, preferred_element_type=F32)
        dk[at, :] += jnp.dot(low, q_t, preferred_element_type=F32)
        dq_t = dq_t + jnp.dot(k_t[:, at], low, preferred_element_type=F32)
    dq[mine, :] = (dq_t * scale).T.astype(BF16)


def main_kernel(
    rows, n_dp, n_tensor, nz, nx,
    q, k, v, g, x_in, gate_weight, gate_bias, lengths,
    dq_out, dk_out, dv_out, weight_out, bias_out,
    qh, kh, vh, gh, parts, part, logits, decay, starts,
    k_t, decay_col, score, grad, dk, dv, col, dq, row_sum, col_sum,
    halo_out, halo_in, low, cols_out, cols_in,
    gate, inbox, wide, term, first, stage, second, x, x_sem,
    in_send, in_recv, own_in, relay_send, relay_recv, small_send, small_recv,
    out_send, out_recv, own_out, halo_send, halo_recv,
    g_send, g_recv, y_send, y_recv, z_send, z_recv, w_send, w_recv, v_send, v_recv,
):
    scale = HEAD ** (-0.5)
    home, window = RING * rows, RING * rows + HALO
    dp, tensor, y, ring = place()
    after, before = lax.rem(dp + RING, n_dp), lax.rem(dp + n_dp - RING, n_dp)
    plane = nz * RING
    xh = dp // plane
    z = lax.rem(dp, plane) // RING
    peers = [(ring_peer(dp, y, s), tensor) for s in range(1, RING)]
    mates = [(dp, lax.rem(tensor + s, n_tensor)) for s in range(1, n_tensor)]
    line = [(xh * plane + lax.rem(z + s, nz) * RING + y, tensor) for s in range(1, nz)]
    planes = [
        (lax.rem(xh + a, nx) * plane + lax.rem(z + b, nz) * RING + y, tensor)
        for a in range(nx)
        for b in range(nz)
    ][1:]
    homes = [
        (ring_peer(dp, y, a), lax.rem(tensor + b, n_tensor)) for a in range(RING) for b in range(n_tensor)
    ][1:]
    x_copy = pltpu.make_async_copy(x_in, x, x_sem)
    x_copy.start()

    def meanwhile():
        x_copy.wait()
        part[...] = lax.dot_general(
            gate_weight[...], x[...], (((1,), (1,)), ((), ())), preferred_element_type=F32
        )

    greet(homes + planes, meanwhile)

    def columns(shard, h):
        return pl.ds(pl.multiple_of(shard * (2 * HEAD) + h * HEAD, HEAD), HEAD)

    def shard_rows(shard, offset=0):
        return pl.ds(pl.multiple_of(offset + shard * rows, rows), rows)

    arrive, own = {}, {}

    def fetch(h, arrays):
        for a in arrays:
            src, dst, ahead = ((k, kh, HALO), (v, vh, HALO), (q, qh, 0), (g, gh, 0))[a]
            at = shard_rows(y, ahead)
            for s in (2, 1, 3):
                arrive[h, a, s] = send(
                    src.at[:, columns(lax.rem(y + s, RING), h)], dst.at[h, at],
                    (in_send, in_recv), h * 12 + a * 3 + s - 1, peers[s - 1],
                )
            own[h, a] = pltpu.make_async_copy(
                src.at[:, columns(y, h)], dst.at[h, at], own_in.at[h * 4 + a]
            )
            own[h, a].start()

    def arrived(h, arrays):
        for a in arrays:
            own[h, a].wait()
            for s in range(1, RING):
                arrive[h, a, s].wait()

    def relay(h):
        tail = pl.ds(home, HALO)
        return [
            send(ref.at[h, tail], ref.at[h, pl.ds(0, HALO)], (relay_send, relay_recv), h * 2 + a, (after, tensor))
            for a, ref in enumerate((kh, vh))
        ]


    small = (small_send, small_recv)
    outs = [
        send(part.at[pl.ds(pl.multiple_of(mate[1] * 8, 8), 8)], parts.at[s], small, s, mate)
        for s, mate in enumerate(mates)
    ]
    fetch(0, (0,))
    eye = lax.broadcasted_iota(jnp.int32, (8, 8), 0) == lax.broadcasted_iota(jnp.int32, (8, 8), 1)
    bias = jnp.sum(
        jnp.where(eye, jnp.broadcast_to(gate_bias[...], (8, 8)), 0.0), axis=1, keepdims=True
    )
    for copy in outs:
        copy.wait()
    logit = part[pl.ds(pl.multiple_of(tensor * 8, 8), 8), :] + bias
    for s in range(n_tensor - 1):
        logit = logit + parts[s]
    logits[2 + y] = logit
    spread = [
        send(logits.at[2 + y], logits.at[2 + y], small, 3 + s, peer) for s, peer in enumerate(peers)
    ]
    fetch(0, (1, 2, 3))
    fetch(1, range(4))
    docs = lengths.shape[1]
    at_0 = lax.broadcasted_iota(jnp.int32, (docs, docs), 0)
    at_1 = lax.broadcasted_iota(jnp.int32, (docs, docs), 1)
    ends = jnp.sum(
        jnp.where(at_1 <= at_0, jnp.broadcast_to(lengths[...], (docs, docs)).astype(F32), 0.0),
        axis=1, keepdims=True,
    ).astype(jnp.int32)
    origin = ring * rows - HALO
    for c in range(home // 512):
        position = ring * rows + c * 512 + lax.broadcasted_iota(jnp.int32, (docs, 512), 1)
        begun = fold(jnp.where(ends <= position, ends, 0), jnp.maximum)
        starts[:, c * 512 : (c + 1) * 512] = jnp.broadcast_to(
            jnp.max(begun, axis=0, keepdims=True) - origin, (8, 512)
        )
    for copy in spread:
        copy.wait()
    ahead = send(logits.at[4:6], logits.at[0:2], small, 6, (after, tensor))
    for h in range(2):
        dk[h] = jnp.zeros((window, HEAD), F32)
        dv[h] = jnp.zeros((window, HEAD), F32)
        col[h] = jnp.zeros((window, HEAD), F32)
    arrived(0, (0, 1))
    relays = relay(0)
    ahead.wait()
    pieces = []
    for s in range(6):
        keep = logits[s]
        keep = -(jnp.maximum(-keep, 0.0) + jnp.log1p(jnp.exp(-jnp.abs(keep))))
        pieces += [keep[:, c * 128 : (c + 1) * 128] * LOG2E for c in range(rows // 128)]
    carry = jnp.zeros((8, 1), F32)
    for i, piece in enumerate(running(pieces, False)):
        decay[:, i * 128 : (i + 1) * 128] = piece + carry
        carry = carry + piece[:, 127:128]
    which = lax.broadcasted_iota(jnp.int32, (8, 512), 0)

    def prepare(h, part_of):
        for c in part_of:
            at = slice(c * 512, (c + 1) * 512)
            k_t[:, at] = kh[h, at, :].T
            mine = jnp.where(which == 2 * y + h, decay[:, at], 0.0)
            decay_col[at, :] = jnp.broadcast_to(jnp.sum(mine, axis=0, keepdims=True), (8, 512)).T

    def tiles(h, low_tile, high_tile):
        def step(t, carry):
            tile_step(
                scale, qh.at[h], kh.at[h], vh.at[h], gh.at[h], k_t, decay_col, starts, score, grad,
                dk.at[h], dv.at[h], col.at[h], dq.at[h], row_sum.at[h], t,
            )
            return carry

        lax.fori_loop(low_tile, high_tile, step, 0)

    leave = []

    def give(src, dst, h, a, shards_of):
        def to(s):
            return pltpu.make_async_remote_copy(
                src_ref=src.at[shard_rows(lax.rem(y + s, RING))],
                dst_ref=dst.at[:, columns(y, h)],
                send_sem=out_send.at[h * 9 + a * 3 + s - 1],
                recv_sem=out_recv.at[h * 9 + a * 3 + s - 1],
                device_id=(ring_peer(dp, y, s), tensor),
                device_id_type=MESH,
            )

        copy = pltpu.make_async_copy(src.at[shard_rows(y)], dst.at[:, columns(y, h)], own_out.at[h * 3 + a])
        for s in (2, 1, 3):
            there = lax.rem(y + s, RING)
            pl.when((there >= shards_of[0]) & (there < shards_of[1]))(to(s).start)
        pl.when((y >= shards_of[0]) & (y < shards_of[1]))(copy.start)
        if shards_of[0] == 0:
            leave.extend([to(1), to(2), to(3), copy])

    back = {}

    def give_halo(h):
        halo_out[h, 0] = (dk[h, :HALO, :] * scale).astype(BF16)
        halo_out[h, 1] = dv[h, :HALO, :].astype(BF16)
        for a in range(2):
            back[h, a] = send(
                halo_out.at[h, a], halo_in.at[h, a], (halo_send, halo_recv), h * 2 + a, (before, tensor)
            )

    grads = ((dk, scale, dk_out), (dv, 1.0, dv_out))
    split = home - HALO
    near, far = (0, split // rows), (split // rows, RING)

    def cast_near(h):
        for a, (of, factor, _) in enumerate(grads):
            low[h, a, :split, :] = (of[h, HALO:home, :] * factor).astype(BF16)

    def give_near(h, arrays=(0, 1)):
        for a in arrays:
            out = grads[a][2]
            give(low.at[h, a], out, h, a + 1, near)

    def give_far(h):
        for a, (of, factor, out) in enumerate(grads):
            back[h, a].wait()
            low[h, a, split:, :] = (
                of[h, home:, :] * factor + halo_in[h, a].astype(F32)
            ).astype(BF16)
            give(low.at[h, a], out, h, a + 1, far)

    def sum_columns(h):
        col_sum[h] = lax.dot_general(
            jnp.ones((8, HEAD), F32), col[h], (((1,), (1,)), ((), ())),
            precision=lax.Precision.HIGHEST, preferred_element_type=F32,
        )

    blocks = window // 512
    halo_blocks = HALO // 512
    half = HALO // TILE
    full = home // TILE
    prepare(0, range(halo_blocks, blocks))
    arrived(0, (2, 3))
    tiles(0, half, full)
    for copy in relays:
        copy.wait()
    prepare(0, range(halo_blocks))
    tiles(0, 0, half // 2)
    arrived(1, (0, 1))
    relays_1 = relay(1)
    tiles(0, half // 2, half)
    give_halo(0)
    cast_near(0)
    give(dq.at[0], dq_out, 0, 0, (0, RING))
    give_near(0)
    sum_columns(0)
    prepare(1, range(halo_blocks, blocks))
    arrived(1, (2, 3))
    tiles(1, half, full)
    for copy in relays_1:
        copy.wait()
    prepare(1, range(halo_blocks))
    give_far(0)
    tiles(1, 0, half)

    sum_columns(1)
    which = lax.broadcasted_iota(jnp.int32, (8, 128), 0)
    crossed = starts[...] < HALO
    over = []
    for h in range(2):
        here = jnp.where(crossed, row_sum[h] - col_sum[h, :, HALO:], 0.0)
        over.append(jnp.broadcast_to(jnp.sum(here, axis=1, keepdims=True), (8, 128)))
    for c in range(HALO // 128):
        at = slice(c * 128, (c + 1) * 128)
        cols_out[:, at] = jnp.where(which == 0, col_sum[0, :, at], col_sum[1, :, at])
    cols_out[:, HALO:] = jnp.where(which == 0, over[0], over[1])
    cols = send(cols_out, cols_in, small, 7, (before, tensor))
    give_halo(1)
    cast_near(1)
    cols.wait()

    pieces, packed = {}, {}
    bias_sum = jnp.zeros((8, 1), F32)
    for h in range(2):
        for c in range(home // 128):
            at = slice(c * 128, (c + 1) * 128)
            piece = row_sum[h, :, at] - col_sum[h, :, HALO + c * 128 : HALO + (c + 1) * 128]
            if c * 128 >= split:
                off = c * 128 - split
                piece = piece - cols_in[h : h + 1, off : off + 128]
            pieces[h, c] = piece
    sums = dict(zip(pieces, running(list(pieces.values()), True)))
    for h in range(2):
        carry = cols_in[h : h + 1, HALO : HALO + 1]
        mine_of = jnp.zeros((8, 1), F32)
        for c in reversed(range(home // 128)):
            shard, off = divmod(c * 128, rows)
            keep = sums[h, c] + carry
            carry = carry + sums[h, c][:, 0:1]
            raw = logits[2 + shard, :, off : off + 128]
            raw = jnp.sum(jnp.where(which == 2 * y + h, raw, 0.0), axis=0, keepdims=True)
            down = jnp.exp(-jnp.abs(raw))
            gate_grad = keep * (jnp.where(raw >= 0, down, 1.0) / (1.0 + down))
            mine_of = mine_of + jnp.sum(gate_grad, axis=1, keepdims=True)
            row = h * (rows // 128) + off // 128
            packed[shard] = jnp.where(which == row, gate_grad, packed.get(shard, 0.0))
        bias_sum = jnp.where(which[:, :1] == 2 * y + h, mine_of, bias_sum)
    for shard in range(RING):
        gate[shard] = packed[shard].astype(BF16).astype(F32)

    slot = tensor * RING + y
    copies = [
        send(gate.at[lax.rem(device[0], RING)], inbox.at[slot], (g_send, g_recv), s, device)
        for s, device in enumerate(homes)
    ]
    give(dq.at[1], dq_out, 1, 0, (0, RING))
    give_near(1, (0,))
    inbox[slot] = gate[y]
    for copy in copies:
        copy.wait()
    for s in range(n_tensor * RING):
        for r in range(8):
            h, c = divmod(r, rows // 128)
            wide[2 * s + h : 2 * s + h + 1, c * 128 : (c + 1) * 128] = inbox[s, r : r + 1, :]
    width = x.shape[1]
    term[:, :width] = jnp.dot(wide[...].astype(BF16), x[...], preferred_element_type=F32)
    for r in range(0, term.shape[0], 8):
        term[r : r + 8, width:] = jnp.broadcast_to(bias_sum, (8, 128))

    copies = [
        send(
            term.at[pl.ds(pl.multiple_of(lax.rem(device[0], RING) * 8, 8), 8)],
            first.at[s], (y_send, y_recv), s, device,
        )
        for s, device in enumerate(peers)
    ]
    give_near(1, (1,))
    here = pl.ds(pl.multiple_of(y * 8, 8), 8)
    part_sum = term[here, :]
    for s, copy in enumerate(copies):
        copy.wait()
        part_sum = part_sum + first[s]
    for c in range(nz):
        stage[c, :, :128] = part_sum[:, c * 128 : (c + 1) * 128]
        stage[c, :, 128:] = part_sum[:, width:]

    copies = [
        send(stage.at[lax.rem(device[0], plane) // RING], second.at[s], (z_send, z_recv), s, device)
        for s, device in enumerate(planes)
    ]
    give_far(1)
    piece = stage[z]
    for s, copy in enumerate(copies):
        copy.wait()
        piece = piece + second[s]
    eye = which == lax.broadcasted_iota(jnp.int32, (8, 128), 1)
    bias_out[...] = jnp.sum(jnp.where(eye, piece[:, 128:], 0.0), axis=0, keepdims=True)[:, :8]

    lanes = pl.ds(pl.multiple_of(z * 128, 128), 128)
    weight_out[here, lanes] = piece[:, :128]
    copies = [
        send(weight_out.at[here, lanes], weight_out.at[here, lanes], (w_send, w_recv), s, device)
        for s, device in enumerate(line)
    ]
    for copy in copies:
        copy.wait()
    copies = [
        send(weight_out.at[here], weight_out.at[here], (v_send, v_recv), s, device)
        for s, device in enumerate(peers)
    ]
    for copy in copies:
        copy.wait()
    for copy in leave:
        copy.wait()


def finish_kernel(*refs):
    count = len(refs) // 3
    ins, outs, held = refs[:count], refs[count : 2 * count], refs[2 * count : 3 * count]
    load, store = refs[3 * count :]
    loads = [pltpu.make_async_copy(ins[i], held[i], load.at[i]) for i in range(count)]
    stores = [pltpu.make_async_copy(held[i], outs[i], store.at[i]) for i in range(count)]
    for copy in loads:
        copy.start()
    for i in range(count):
        loads[i].wait()
        stores[i].start()
    for copy in stores:
        copy.wait()


def finish(*arrays):
    hbm = pl.BlockSpec(memory_space=pl.ANY)
    return pl.pallas_call(
        finish_kernel,
        out_shape=tuple(jax.ShapeDtypeStruct(a.shape, a.dtype) for a in arrays),
        in_specs=[hbm] * len(arrays),
        out_specs=(hbm,) * len(arrays),
        scratch_shapes=[pltpu.VMEM(a.shape, a.dtype) for a in arrays]
        + [pltpu.SemaphoreType.DMA((len(arrays),))] * 2,
        compiler_params=pltpu.CompilerParams(vmem_limit_bytes=56 * 2**20),
        name="finish",
    )(*arrays)


def shards(n_dp, n_tensor, q, k, v, g, x, gate_weight, gate_bias, doc_lengths):
    rows, width = q.shape
    home, window = RING * rows, RING * rows + HALO
    heads = 8 * n_tensor
    nx = 2
    nz = n_dp // (RING * nx)
    assert width == 128 * nz and heads == 8 * RING and rows == 512
    chunks = BAND // TILE
    hbm, vmem = pl.BlockSpec(memory_space=pl.ANY), pl.BlockSpec(memory_space=pltpu.VMEM)

    def dma(*sizes):
        return [pltpu.SemaphoreType.DMA((size,)) for size in sizes]

    out = jax.ShapeDtypeStruct((rows, width), BF16)
    pair = [pltpu.VMEM((2, window, HEAD), F32)]
    dq, dk, dv, weight, bias = pl.pallas_call(
        functools.partial(main_kernel, rows, n_dp, n_tensor, nz, nx),
        out_shape=(
            out, out, out,
            jax.ShapeDtypeStruct((heads, width), F32),
            jax.ShapeDtypeStruct((1, 8), F32),
        ),
        in_specs=[hbm] * 5 + [vmem] * 3,
        out_specs=(hbm, hbm, hbm, vmem, vmem),
        scratch_shapes=[
            pltpu.VMEM((2, home, HEAD), BF16),
            pltpu.VMEM((2, window, HEAD), BF16),
            pltpu.VMEM((2, window, HEAD), BF16),
            pltpu.VMEM((2, home, HEAD), BF16),
            pltpu.VMEM((n_tensor - 1, 8, rows), F32),
            pltpu.VMEM((heads, rows), F32),
            pltpu.VMEM((6, 8, rows), F32),
            pltpu.VMEM((8, window), F32),
            pltpu.VMEM((8, home), jnp.int32),
            pltpu.VMEM((HEAD, window), BF16),
            pltpu.VMEM((window, 8), F32),
            pltpu.VMEM((chunks, TILE, TILE), F32),
            pltpu.VMEM((chunks, TILE, TILE), F32),
            *(pair * 3),
            pltpu.VMEM((2, home, HEAD), BF16),
            pltpu.VMEM((2, 8, home), F32),
            pltpu.VMEM((2, 8, window), F32),
            pltpu.VMEM((2, 2, HALO, HEAD), BF16),
            pltpu.VMEM((2, 2, HALO, HEAD), BF16),
            pltpu.VMEM((2, 2, home, HEAD), BF16),
            pltpu.VMEM((8, HALO + 128), F32),
            pltpu.VMEM((8, HALO + 128), F32),
            pltpu.VMEM((RING, 8, 128), F32),
            pltpu.VMEM((n_tensor * RING, 8, 128), F32),
            pltpu.VMEM((heads, rows), F32),
            pltpu.VMEM((heads, width + 128), F32),
            pltpu.VMEM((3, 8, width + 128), F32),
            pltpu.VMEM((nz, 8, 256), F32),
            pltpu.VMEM((nx * nz - 1, 8, 256), F32),
            pltpu.VMEM((rows, width), BF16),
            pltpu.SemaphoreType.DMA,
            *dma(24, 24, 8, 4, 4, 8, 8),
            *dma(18, 18, 6, 4, 4),
            *dma(*[n_tensor * RING - 1] * 2, 3, 3, *[nx * nz - 1] * 2, nz - 1, nz - 1, 3, 3),
        ],
        compiler_params=pltpu.CompilerParams(
            collective_id=0, has_side_effects=True, vmem_limit_bytes=56 * 2**20
        ),
        name="main",
    )(q, k, v, g, x, gate_weight.T, gate_bias.reshape(1, 8), doc_lengths.reshape(1, -1))
    dq, dk, dv, weight, bias = finish(dq, dk, dv, weight, bias)
    return dq, dk, dv, weight.T, bias.reshape(8)


def solution(mesh):
    return jax.shard_map(
        functools.partial(shards, mesh.shape["dp"], mesh.shape["tensor"]),
        mesh=mesh,
        in_specs=(
            P("dp", "tensor"),
            P("dp", "tensor"),
            P("dp", "tensor"),
            P("dp", "tensor"),
            P("dp", "tensor"),
            P("tensor", None),
            P("tensor"),
            P(),
        ),
        out_specs=(
            P("dp", "tensor"),
            P("dp", "tensor"),
            P("dp", "tensor"),
            P("tensor", None),
            P("tensor"),
        ),
        check_vma=False,
    )
```

```python
import functools
import math

import jax
import jax.numpy as jnp
from jax import lax
from jax.experimental import pallas as pl
from jax.experimental.pallas import tpu as pltpu
from jax.sharding import PartitionSpec as P

RING = 4
HALO = 1024
HEAD = 128
TILE = 256
BAND = HALO + TILE
LOG2E = math.log2(math.e)
DEAD = -1e30
MESH = pl.DeviceIdType.MESH
F32 = jnp.float32
BF16 = jnp.bfloat16


def place():
    dp, tensor = lax.axis_index("dp"), lax.axis_index("tensor")
    y = lax.rem(dp, RING)
    return dp, tensor, y, dp - y


def ring_peer(dp, y, step):
    return dp - y + lax.rem(y + step, RING)


def greet(devices, meanwhile):
    barrier = pltpu.get_barrier_semaphore()
    for device in devices:
        pl.semaphore_signal(barrier, inc=1, device_id=device, device_id_type=MESH)
    meanwhile()
    pl.semaphore_wait(barrier, len(devices))


def send(src, dst, sems, at, device):
    copy = pltpu.make_async_remote_copy(
        src_ref=src,
        dst_ref=dst,
        send_sem=sems[0].at[at],
        recv_sem=sems[1].at[at],
        device_id=device,
        device_id_type=MESH,
    )
    copy.start()
    return copy


def fold(x, combine):
    out = x[:8]
    for r in range(8, x.shape[0], 8):
        out = combine(out, x[r : r + 8])
    return out


def running(chunks, later):
    a = lax.broadcasted_iota(jnp.int32, (128, 128), 0)
    b = lax.broadcasted_iota(jnp.int32, (128, 128), 1)
    ones = jnp.where(a >= b if later else a <= b, 1.0, 0.0).astype(F32)
    sums = jnp.dot(
        jnp.concatenate(chunks), ones, precision=lax.Precision.HIGHEST, preferred_element_type=F32
    )
    return [sums[8 * i : 8 * i + 8] for i in range(len(chunks))]


def tile_step(scale, q, k, v, g, k_t, decay_col, starts, score, grad, dk, dv, col, dq, rows_sum, t, saved=None):
    chunks = BAND // TILE
    nt = (((1,), (1,)), ((), ()))
    base = pl.multiple_of(t * TILE, TILE)
    mine = pl.ds(base, TILE)
    q_t, g_t = q[mine, :], g[mine, :]
    first = starts[0:1, mine] - base
    key_at = lax.broadcasted_iota(jnp.int32, (TILE, TILE), 0)
    top = jnp.full((8, TILE), DEAD, F32)
    for c in range(chunks):
        at = pl.ds(base + c * TILE, TILE)
        s = lax.dot_general(k[at, :], q_t, nt, preferred_element_type=F32)
        s = s * (scale * LOG2E) - decay_col[at, 0:1]
        live = key_at >= first - c * TILE
        if c == chunks - 1:
            live = live & (key_at <= lax.broadcasted_iota(jnp.int32, (TILE, TILE), 1))
        s = jnp.where(live, s, DEAD)
        score[c] = s
        top = jnp.maximum(top, fold(s, jnp.maximum))
    top = jnp.max(top, axis=0, keepdims=True)
    total = jnp.zeros((8, TILE), F32)
    delta = jnp.zeros((8, TILE), F32)
    for c in range(chunks):
        at = pl.ds(base + c * TILE, TILE)
        w = jnp.exp2(score[c] - top)
        d = lax.dot_general(v[at, :], g_t, nt, preferred_element_type=F32)
        score[c] = w
        grad[c] = d
        total = total + fold(w, jnp.add)
        delta = delta + fold(w * d, jnp.add)
    total = jnp.sum(total, axis=0, keepdims=True)
    inverse = 1.0 / total
    delta = jnp.sum(delta, axis=0, keepdims=True) * inverse
    rows_sum[:, mine] = jnp.broadcast_to(delta - delta * (total * inverse), (8, TILE))
    dq_t = jnp.zeros((HEAD, TILE), F32)
    for c in range(chunks):
        at = pl.ds(base + c * TILE, TILE)
        p = score[c] * inverse
        ds = p * (grad[c] - delta)
        low = ds.astype(BF16)
        col[at, :] += ds[:, :HEAD] + ds[:, HEAD:]
        if saved is not None:
            saved[0][t, c] = p.astype(BF16)
            saved[1][t, c] = low
            continue
        dv[at, :] += jnp.dot(p.astype(BF16), g_t, preferred_element_type=F32)
        dk[at, :] += jnp.dot(low, q_t, preferred_element_type=F32)
        dq_t = dq_t + jnp.dot(k_t[:, at], low, preferred_element_type=F32)
    if saved is None:
        dq[mine, :] = (dq_t * scale).T.astype(BF16)


def tile_products(scale, q, g, k_t, dk, dv, dq, saved, t):
    base = pl.multiple_of(t * TILE, TILE)
    mine = pl.ds(base, TILE)
    q_t, g_t = q[mine, :], g[mine, :]
    dq_t = jnp.zeros((HEAD, TILE), F32)
    for c in range(BAND // TILE):
        at = pl.ds(base + c * TILE, TILE)
        low = saved[1][t, c]
        dv[at, :] += jnp.dot(saved[0][t, c], g_t, preferred_element_type=F32)
        dk[at, :] += jnp.dot(low, q_t, preferred_element_type=F32)
        dq_t = dq_t + jnp.dot(k_t[:, at], low, preferred_element_type=F32)
    dq[mine, :] = (dq_t * scale).T.astype(BF16)


def main_kernel(
    rows, n_dp, n_tensor, nz, nx,
    q, k, v, g, x_in, gate_weight, gate_bias, lengths,
    dq_out, dk_out, dv_out, weight_out, bias_out,
    qh, kh, vh, gh, parts, part, logits, decay, starts,
    k_t, decay_col, score, grad, dk, dv, col, dq, row_sum, col_sum,
    halo_out, halo_in, low, cols_out, cols_in,
    gate, inbox, wide, term, stage, first, second, x, x_sem, saved_p, saved_s,
    in_send, in_recv, own_in, relay_send, relay_recv, small_send, small_recv,
    out_send, out_recv, own_out, halo_send, halo_recv,
    g_send, g_recv, z_send, z_recv, y_send, y_recv, w_send, w_recv,
):
    scale = HEAD ** (-0.5)
    home, window = RING * rows, RING * rows + HALO
    dp, tensor, y, ring = place()
    after, before = lax.rem(dp + RING, n_dp), lax.rem(dp + n_dp - RING, n_dp)
    plane = nz * RING
    xh = dp // plane
    z = lax.rem(dp, plane) // RING
    peers = [(ring_peer(dp, y, s), tensor) for s in range(1, RING)]
    mates = [(dp, lax.rem(tensor + s, n_tensor)) for s in range(1, n_tensor)]
    line = [(xh * plane + lax.rem(z + s, nz) * RING + y, tensor) for s in range(1, nz)]
    sides = [
        (lax.rem(xh + a, nx) * plane + z * RING + lax.rem(y + b, RING), tensor)
        for a in range(nx)
        for b in range(RING)
    ][1:]
    homes = [
        (ring_peer(dp, y, a), lax.rem(tensor + b, n_tensor)) for a in range(RING) for b in range(n_tensor)
    ][1:]
    x_copy = pltpu.make_async_copy(x_in, x, x_sem)
    x_copy.start()

    def meanwhile():
        x_copy.wait()
        part[...] = lax.dot_general(
            gate_weight[...], x[...], (((1,), (1,)), ((), ())), preferred_element_type=F32
        )

    greet(homes + line + sides[RING - 1 :] + [(after, tensor), (before, tensor)], meanwhile)

    def columns(shard, h):
        return pl.ds(pl.multiple_of(shard * (2 * HEAD) + h * HEAD, HEAD), HEAD)

    def shard_rows(shard, offset=0):
        return pl.ds(pl.multiple_of(offset + shard * rows, rows), rows)

    arrive, own = {}, {}

    def fetch(h, arrays):
        for a in arrays:
            src, dst, ahead = ((k, kh, HALO), (v, vh, HALO), (q, qh, 0), (g, gh, 0))[a]
            at = shard_rows(y, ahead)
            for s in (2, 1, 3):
                arrive[h, a, s] = send(
                    src.at[:, columns(lax.rem(y + s, RING), h)], dst.at[h, at],
                    (in_send, in_recv), h * 12 + a * 3 + s - 1, peers[s - 1],
                )
            own[h, a] = pltpu.make_async_copy(
                src.at[:, columns(y, h)], dst.at[h, at], own_in.at[h * 4 + a]
            )
            own[h, a].start()

    def arrived(h, arrays):
        for a in arrays:
            own[h, a].wait()
            for s in range(1, RING):
                arrive[h, a, s].wait()

    def relay(h):
        tail = pl.ds(home, HALO)
        return [
            send(ref.at[h, tail], ref.at[h, pl.ds(0, HALO)], (relay_send, relay_recv), h * 2 + a, (after, tensor))
            for a, ref in enumerate((kh, vh))
        ]


    small = (small_send, small_recv)
    outs = [
        send(part.at[pl.ds(pl.multiple_of(mate[1] * 8, 8), 8)], parts.at[s], small, s, mate)
        for s, mate in enumerate(mates)
    ]
    fetch(0, (0,))
    eye = lax.broadcasted_iota(jnp.int32, (8, 8), 0) == lax.broadcasted_iota(jnp.int32, (8, 8), 1)
    bias = jnp.sum(
        jnp.where(eye, jnp.broadcast_to(gate_bias[...], (8, 8)), 0.0), axis=1, keepdims=True
    )
    for copy in outs:
        copy.wait()
    logit = part[pl.ds(pl.multiple_of(tensor * 8, 8), 8), :] + bias
    for s in range(n_tensor - 1):
        logit = logit + parts[s]
    logits[2 + y] = logit
    spread = [
        send(logits.at[2 + y], logits.at[2 + y], small, 3 + s, peer) for s, peer in enumerate(peers)
    ]
    fetch(0, (1, 2, 3))
    fetch(1, range(4))
    docs = lengths.shape[1]
    at_0 = lax.broadcasted_iota(jnp.int32, (docs, docs), 0)
    at_1 = lax.broadcasted_iota(jnp.int32, (docs, docs), 1)
    ends = jnp.sum(
        jnp.where(at_1 <= at_0, jnp.broadcast_to(lengths[...], (docs, docs)).astype(F32), 0.0),
        axis=1, keepdims=True,
    ).astype(jnp.int32)
    origin = ring * rows - HALO
    for c in range(home // 512):
        position = ring * rows + c * 512 + lax.broadcasted_iota(jnp.int32, (docs, 512), 1)
        begun = fold(jnp.where(ends <= position, ends, 0), jnp.maximum)
        starts[:, c * 512 : (c + 1) * 512] = jnp.broadcast_to(
            jnp.max(begun, axis=0, keepdims=True) - origin, (8, 512)
        )
    for copy in spread:
        copy.wait()
    ahead = send(logits.at[4:6], logits.at[0:2], small, 6, (after, tensor))
    for h in range(2):
        dk[h] = jnp.zeros((window, HEAD), F32)
        dv[h] = jnp.zeros((window, HEAD), F32)
        col[h] = jnp.zeros((window, HEAD), F32)
    arrived(0, (0, 1))
    relays = relay(0)
    ahead.wait()
    pieces = []
    for s in range(6):
        keep = logits[s]
        keep = -(jnp.maximum(-keep, 0.0) + jnp.log1p(jnp.exp(-jnp.abs(keep))))
        pieces += [keep[:, c * 128 : (c + 1) * 128] * LOG2E for c in range(rows // 128)]
    carry = jnp.zeros((8, 1), F32)
    for i, piece in enumerate(running(pieces, False)):
        decay[:, i * 128 : (i + 1) * 128] = piece + carry
        carry = carry + piece[:, 127:128]
    which = lax.broadcasted_iota(jnp.int32, (8, 512), 0)

    def prepare(h, part_of):
        for c in part_of:
            at = slice(c * 512, (c + 1) * 512)
            k_t[:, at] = kh[h, at, :].T
            mine = jnp.where(which == 2 * y + h, decay[:, at], 0.0)
            decay_col[at, :] = jnp.broadcast_to(jnp.sum(mine, axis=0, keepdims=True), (8, 512)).T

    def tiles(h, low_tile, high_tile, saved=None):
        def step(t, carry):
            tile_step(
                scale, qh.at[h], kh.at[h], vh.at[h], gh.at[h], k_t, decay_col, starts, score, grad,
                dk.at[h], dv.at[h], col.at[h], dq.at[h], row_sum.at[h], t, saved,
            )
            return carry

        lax.fori_loop(low_tile, high_tile, step, 0)

    def products(h, low_tile, high_tile, saved):
        def step(t, carry):
            tile_products(scale, qh.at[h], gh.at[h], k_t, dk.at[h], dv.at[h], dq.at[h], saved, t)
            return carry

        lax.fori_loop(low_tile, high_tile, step, 0)

    leave = []

    def give(src, dst, h, a, shards_of):
        def to(s):
            return pltpu.make_async_remote_copy(
                src_ref=src.at[shard_rows(lax.rem(y + s, RING))],
                dst_ref=dst.at[:, columns(y, h)],
                send_sem=out_send.at[h * 9 + a * 3 + s - 1],
                recv_sem=out_recv.at[h * 9 + a * 3 + s - 1],
                device_id=(ring_peer(dp, y, s), tensor),
                device_id_type=MESH,
            )

        copy = pltpu.make_async_copy(src.at[shard_rows(y)], dst.at[:, columns(y, h)], own_out.at[h * 3 + a])
        for s in (2, 1, 3):
            there = lax.rem(y + s, RING)
            pl.when((there >= shards_of[0]) & (there < shards_of[1]))(to(s).start)
        pl.when((y >= shards_of[0]) & (y < shards_of[1]))(copy.start)
        if shards_of[0] == 0:
            leave.extend([to(1), to(2), to(3), copy])

    back = {}

    def give_halo(h):
        halo_out[h, 0] = (dk[h, :HALO, :] * scale).astype(BF16)
        halo_out[h, 1] = dv[h, :HALO, :].astype(BF16)
        for a in range(2):
            back[h, a] = send(
                halo_out.at[h, a], halo_in.at[h, a], (halo_send, halo_recv), h * 2 + a, (before, tensor)
            )

    grads = ((dk, scale, dk_out), (dv, 1.0, dv_out))
    split = home - HALO
    near, far = (0, split // rows), (split // rows, RING)

    def cast_near(h):
        for a, (of, factor, _) in enumerate(grads):
            low[h, a, :split, :] = (of[h, HALO:home, :] * factor).astype(BF16)

    def give_near(h, arrays=(0, 1)):
        for a in arrays:
            out = grads[a][2]
            give(low.at[h, a], out, h, a + 1, near)

    def give_far(h):
        for a, (of, factor, out) in enumerate(grads):
            back[h, a].wait()
            low[h, a, split:, :] = (
                of[h, home:, :] * factor + halo_in[h, a].astype(F32)
            ).astype(BF16)
            give(low.at[h, a], out, h, a + 1, far)

    def sum_columns(h):
        col_sum[h] = lax.dot_general(
            jnp.ones((8, HEAD), F32), col[h], (((1,), (1,)), ((), ())),
            precision=lax.Precision.HIGHEST, preferred_element_type=F32,
        )

    blocks = window // 512
    halo_blocks = HALO // 512
    half = HALO // TILE
    full = home // TILE
    prepare(0, range(halo_blocks, blocks))
    arrived(0, (2, 3))
    tiles(0, half, full)
    for copy in relays:
        copy.wait()
    prepare(0, range(halo_blocks))
    tiles(0, 0, half // 2)
    arrived(1, (0, 1))
    relays_1 = relay(1)
    tiles(0, half // 2, half)
    give_halo(0)
    cast_near(0)
    give(dq.at[0], dq_out, 0, 0, (0, RING))
    give_near(0)
    sum_columns(0)
    prepare(1, range(halo_blocks, blocks))
    arrived(1, (2, 3))
    saved = (saved_p, saved_s)
    tiles(1, half, full, saved)
    for copy in relays_1:
        copy.wait()
    prepare(1, range(halo_blocks))
    tiles(1, 0, half, saved)

    sum_columns(1)
    which = lax.broadcasted_iota(jnp.int32, (8, 128), 0)
    crossed = starts[...] < HALO
    over = []
    for h in range(2):
        here = jnp.where(crossed, row_sum[h] - col_sum[h, :, HALO:], 0.0)
        over.append(jnp.broadcast_to(jnp.sum(here, axis=1, keepdims=True), (8, 128)))
    for c in range(HALO // 128):
        at = slice(c * 128, (c + 1) * 128)
        cols_out[:, at] = jnp.where(which == 0, col_sum[0, :, at], col_sum[1, :, at])
    cols_out[:, HALO:] = jnp.where(which == 0, over[0], over[1])
    cols = send(cols_out, cols_in, small, 7, (before, tensor))
    give_far(0)
    products(1, 0, half, saved)
    give_halo(1)
    cols.wait()

    pieces, packed = {}, {}
    bias_sum = jnp.zeros((8, 1), F32)
    for h in range(2):
        for c in range(home // 128):
            at = slice(c * 128, (c + 1) * 128)
            piece = row_sum[h, :, at] - col_sum[h, :, HALO + c * 128 : HALO + (c + 1) * 128]
            if c * 128 >= split:
                off = c * 128 - split
                piece = piece - cols_in[h : h + 1, off : off + 128]
            pieces[h, c] = piece
    sums = dict(zip(pieces, running(list(pieces.values()), True)))
    for h in range(2):
        carry = cols_in[h : h + 1, HALO : HALO + 1]
        mine_of = jnp.zeros((8, 1), F32)
        for c in reversed(range(home // 128)):
            shard, off = divmod(c * 128, rows)
            keep = sums[h, c] + carry
            carry = carry + sums[h, c][:, 0:1]
            raw = logits[2 + shard, :, off : off + 128]
            raw = jnp.sum(jnp.where(which == 2 * y + h, raw, 0.0), axis=0, keepdims=True)
            down = jnp.exp(-jnp.abs(raw))
            gate_grad = keep * (jnp.where(raw >= 0, down, 1.0) / (1.0 + down))
            mine_of = mine_of + jnp.sum(gate_grad, axis=1, keepdims=True)
            row = h * (rows // 128) + off // 128
            packed[shard] = jnp.where(which == row, gate_grad, packed.get(shard, 0.0))
        bias_sum = jnp.where(which[:, :1] == 2 * y + h, mine_of, bias_sum)
    for shard in range(RING):
        gate[shard] = packed[shard].astype(BF16).astype(F32)

    slot = tensor * RING + y
    copies = [
        send(gate.at[lax.rem(device[0], RING)], inbox.at[slot], (g_send, g_recv), s, device)
        for s, device in enumerate(homes)
    ]
    products(1, half, full, saved)
    give(dq.at[1], dq_out, 1, 0, (0, RING))
    cast_near(1)
    give_near(1, (0,))
    inbox[slot] = gate[y]
    for copy in copies:
        copy.wait()
    for s in range(n_tensor * RING):
        for r in range(8):
            h, c = divmod(r, rows // 128)
            wide[2 * s + h : 2 * s + h + 1, c * 128 : (c + 1) * 128] = inbox[s, r : r + 1, :]
    term[...] = jnp.dot(wide[...].astype(BF16), x[...], preferred_element_type=F32)
    for c in range(nz):
        stage[c, : term.shape[0], :] = term[:, c * 128 : (c + 1) * 128]
        stage[c, term.shape[0] :, :] = jnp.broadcast_to(bias_sum, (8, 128))
    copies = [
        send(stage.at[lax.rem(device[0], plane) // RING], first.at[s], (z_send, z_recv), s, device)
        for s, device in enumerate(line)
    ]
    piece = stage[z]
    for s, copy in enumerate(copies):
        copy.wait()
        piece = piece + first[s]

    stage[z] = piece
    copies = [
        send(stage.at[z], second.at[s], (y_send, y_recv), s, device) for s, device in enumerate(sides)
    ]
    give_near(1, (1,))
    give_far(1)
    for s, copy in enumerate(copies):
        copy.wait()
        piece = piece + second[s]
    eye = which == lax.broadcasted_iota(jnp.int32, (8, 128), 1)
    bias_out[...] = jnp.sum(jnp.where(eye, piece[term.shape[0] :], 0.0), axis=0, keepdims=True)[:, :8]

    lanes = pl.ds(pl.multiple_of(z * 128, 128), 128)
    weight_out[:, lanes] = piece[: term.shape[0]]
    copies = [
        send(weight_out.at[:, lanes], weight_out.at[:, lanes], (w_send, w_recv), s, device)
        for s, device in enumerate(line)
    ]
    for copy in copies:
        copy.wait()
    for copy in leave:
        copy.wait()


def finish_kernel(*refs):
    count = len(refs) // 3
    ins, outs, held = refs[:count], refs[count : 2 * count], refs[2 * count : 3 * count]
    load, store = refs[3 * count :]
    loads = [pltpu.make_async_copy(ins[i], held[i], load.at[i]) for i in range(count)]
    stores = [pltpu.make_async_copy(held[i], outs[i], store.at[i]) for i in range(count)]
    for copy in loads:
        copy.start()
    for i in range(count):
        loads[i].wait()
        stores[i].start()
    for copy in stores:
        copy.wait()


def finish(*arrays):
    hbm = pl.BlockSpec(memory_space=pl.ANY)
    return pl.pallas_call(
        finish_kernel,
        out_shape=tuple(jax.ShapeDtypeStruct(a.shape, a.dtype) for a in arrays),
        in_specs=[hbm] * len(arrays),
        out_specs=(hbm,) * len(arrays),
        scratch_shapes=[pltpu.VMEM(a.shape, a.dtype) for a in arrays]
        + [pltpu.SemaphoreType.DMA((len(arrays),))] * 2,
        compiler_params=pltpu.CompilerParams(vmem_limit_bytes=56 * 2**20),
        name="finish",
    )(*arrays)


def shards(n_dp, n_tensor, q, k, v, g, x, gate_weight, gate_bias, doc_lengths):
    rows, width = q.shape
    home, window = RING * rows, RING * rows + HALO
    heads = 8 * n_tensor
    nx = 2
    nz = n_dp // (RING * nx)
    assert width == 128 * nz and heads == 8 * RING and rows == 512
    chunks = BAND // TILE
    hbm, vmem = pl.BlockSpec(memory_space=pl.ANY), pl.BlockSpec(memory_space=pltpu.VMEM)

    def dma(*sizes):
        return [pltpu.SemaphoreType.DMA((size,)) for size in sizes]

    out = jax.ShapeDtypeStruct((rows, width), BF16)
    pair = [pltpu.VMEM((2, window, HEAD), F32)]
    dq, dk, dv, weight, bias = pl.pallas_call(
        functools.partial(main_kernel, rows, n_dp, n_tensor, nz, nx),
        out_shape=(
            out, out, out,
            jax.ShapeDtypeStruct((heads, width), F32),
            jax.ShapeDtypeStruct((1, 8), F32),
        ),
        in_specs=[hbm] * 5 + [vmem] * 3,
        out_specs=(hbm, hbm, hbm, vmem, vmem),
        scratch_shapes=[
            pltpu.VMEM((2, home, HEAD), BF16),
            pltpu.VMEM((2, window, HEAD), BF16),
            pltpu.VMEM((2, window, HEAD), BF16),
            pltpu.VMEM((2, home, HEAD), BF16),
            pltpu.VMEM((n_tensor - 1, 8, rows), F32),
            pltpu.VMEM((heads, rows), F32),
            pltpu.VMEM((6, 8, rows), F32),
            pltpu.VMEM((8, window), F32),
            pltpu.VMEM((8, home), jnp.int32),
            pltpu.VMEM((HEAD, window), BF16),
            pltpu.VMEM((window, 8), F32),
            pltpu.VMEM((chunks, TILE, TILE), F32),
            pltpu.VMEM((chunks, TILE, TILE), F32),
            *(pair * 3),
            pltpu.VMEM((2, home, HEAD), BF16),
            pltpu.VMEM((2, 8, home), F32),
            pltpu.VMEM((2, 8, window), F32),
            pltpu.VMEM((2, 2, HALO, HEAD), BF16),
            pltpu.VMEM((2, 2, HALO, HEAD), BF16),
            pltpu.VMEM((2, 2, home, HEAD), BF16),
            pltpu.VMEM((8, HALO + 128), F32),
            pltpu.VMEM((8, HALO + 128), F32),
            pltpu.VMEM((RING, 8, 128), F32),
            pltpu.VMEM((n_tensor * RING, 8, 128), F32),
            pltpu.VMEM((heads, rows), F32),
            pltpu.VMEM((heads, width), F32),
            pltpu.VMEM((nz, heads + 8, 128), F32),
            pltpu.VMEM((nz - 1, heads + 8, 128), F32),
            pltpu.VMEM((nx * RING - 1, heads + 8, 128), F32),
            pltpu.VMEM((rows, width), BF16),
            pltpu.SemaphoreType.DMA,
            *([pltpu.VMEM((home // TILE, chunks, TILE, TILE), BF16)] * 2),
            *dma(24, 24, 8, 4, 4, 8, 8),
            *dma(18, 18, 6, 4, 4),
            *dma(*[n_tensor * RING - 1] * 2, *[nz - 1] * 2, *[nx * RING - 1] * 2, *[nz - 1] * 2),
        ],
        compiler_params=pltpu.CompilerParams(
            collective_id=0, has_side_effects=True, vmem_limit_bytes=56 * 2**20
        ),
        name="main",
    )(q, k, v, g, x, gate_weight.T, gate_bias.reshape(1, 8), doc_lengths.reshape(1, -1))
    dq, dk, dv, weight, bias = finish(dq, dk, dv, weight, bias)
    return dq, dk, dv, weight.T, bias.reshape(8)


def solution(mesh):
    return jax.shard_map(
        functools.partial(shards, mesh.shape["dp"], mesh.shape["tensor"]),
        mesh=mesh,
        in_specs=(
            P("dp", "tensor"),
            P("dp", "tensor"),
            P("dp", "tensor"),
            P("dp", "tensor"),
            P("dp", "tensor"),
            P("tensor", None),
            P("tensor"),
            P(),
        ),
        out_specs=(
            P("dp", "tensor"),
            P("dp", "tensor"),
            P("dp", "tensor"),
            P("tensor", None),
            P("tensor"),
        ),
        check_vma=False,
    )
```

```python
import functools
import math

import jax
import jax.numpy as jnp
from jax import lax
from jax.experimental import pallas as pl
from jax.experimental.pallas import tpu as pltpu
from jax.sharding import PartitionSpec as P

RING = 4
HALO = 1024
HEAD = 128
TILE = 256
BAND = HALO + TILE
LOG2E = math.log2(math.e)
DEAD = -1e30
MESH = pl.DeviceIdType.MESH
F32 = jnp.float32
BF16 = jnp.bfloat16


def place():
    dp, tensor = lax.axis_index("dp"), lax.axis_index("tensor")
    y = lax.rem(dp, RING)
    return dp, tensor, y, dp - y


def ring_peer(dp, y, step):
    return dp - y + lax.rem(y + step, RING)


def greet(devices, meanwhile):
    barrier = pltpu.get_barrier_semaphore()
    for device in devices:
        pl.semaphore_signal(barrier, inc=1, device_id=device, device_id_type=MESH)
    meanwhile()
    pl.semaphore_wait(barrier, len(devices))


def send(src, dst, sems, at, device):
    copy = pltpu.make_async_remote_copy(
        src_ref=src,
        dst_ref=dst,
        send_sem=sems[0].at[at],
        recv_sem=sems[1].at[at],
        device_id=device,
        device_id_type=MESH,
    )
    copy.start()
    return copy


def fold(x, combine):
    out = x[:8]
    for r in range(8, x.shape[0], 8):
        out = combine(out, x[r : r + 8])
    return out


def running(chunks, later):
    a = lax.broadcasted_iota(jnp.int32, (128, 128), 0)
    b = lax.broadcasted_iota(jnp.int32, (128, 128), 1)
    ones = jnp.where(a >= b if later else a <= b, 1.0, 0.0).astype(F32)
    sums = jnp.dot(
        jnp.concatenate(chunks), ones, precision=lax.Precision.HIGHEST, preferred_element_type=F32
    )
    return [sums[8 * i : 8 * i + 8] for i in range(len(chunks))]


def tile_step(scale, q, k, v, g, k_t, decay_col, starts, score, grad, dk, dv, col, dq, rows_sum, t, saved=None):
    chunks = BAND // TILE
    nt = (((1,), (1,)), ((), ()))
    base = pl.multiple_of(t * TILE, TILE)
    mine = pl.ds(base, TILE)
    q_t, g_t = q[mine, :], g[mine, :]
    first = starts[0:1, mine] - base
    key_at = lax.broadcasted_iota(jnp.int32, (TILE, TILE), 0)
    top = jnp.full((8, TILE), DEAD, F32)
    for c in range(chunks):
        at = pl.ds(base + c * TILE, TILE)
        s = lax.dot_general(k[at, :], q_t, nt, preferred_element_type=F32)
        s = s * (scale * LOG2E) - decay_col[at, 0:1]
        live = key_at >= first - c * TILE
        if c == chunks - 1:
            live = live & (key_at <= lax.broadcasted_iota(jnp.int32, (TILE, TILE), 1))
        s = jnp.where(live, s, DEAD)
        score[c] = s
        top = jnp.maximum(top, fold(s, jnp.maximum))
    top = jnp.max(top, axis=0, keepdims=True)
    total = jnp.zeros((8, TILE), F32)
    delta = jnp.zeros((8, TILE), F32)
    for c in range(chunks):
        at = pl.ds(base + c * TILE, TILE)
        w = jnp.exp2(score[c] - top)
        d = lax.dot_general(v[at, :], g_t, nt, preferred_element_type=F32)
        score[c] = w
        grad[c] = d
        total = total + fold(w, jnp.add)
        delta = delta + fold(w * d, jnp.add)
    total = jnp.sum(total, axis=0, keepdims=True)
    inverse = 1.0 / total
    delta = jnp.sum(delta, axis=0, keepdims=True) * inverse
    rows_sum[:, mine] = jnp.broadcast_to(delta - delta * (total * inverse), (8, TILE))
    dq_t = jnp.zeros((HEAD, TILE), F32)
    for c in range(chunks):
        at = pl.ds(base + c * TILE, TILE)
        p = score[c] * inverse
        ds = p * (grad[c] - delta)
        low = ds.astype(BF16)
        col[at, :] += ds[:, :HEAD] + ds[:, HEAD:]
        if saved is not None:
            saved[0][t, c] = p.astype(BF16)
            saved[1][t, c] = low
            continue
        dv[at, :] += jnp.dot(p.astype(BF16), g_t, preferred_element_type=F32)
        dk[at, :] += jnp.dot(low, q_t, preferred_element_type=F32)
        dq_t = dq_t + jnp.dot(k_t[:, at], low, preferred_element_type=F32)
    if saved is None:
        dq[mine, :] = (dq_t * scale).T.astype(BF16)


def tile_products(scale, q, g, k_t, dk, dv, dq, saved, t):
    base = pl.multiple_of(t * TILE, TILE)
    mine = pl.ds(base, TILE)
    q_t, g_t = q[mine, :], g[mine, :]
    dq_t = jnp.zeros((HEAD, TILE), F32)
    for c in range(BAND // TILE):
        at = pl.ds(base + c * TILE, TILE)
        low = saved[1][t, c]
        dv[at, :] += jnp.dot(saved[0][t, c], g_t, preferred_element_type=F32)
        dk[at, :] += jnp.dot(low, q_t, preferred_element_type=F32)
        dq_t = dq_t + jnp.dot(k_t[:, at], low, preferred_element_type=F32)
    dq[mine, :] = (dq_t * scale).T.astype(BF16)


def main_kernel(
    rows, n_dp, n_tensor, nz, nx,
    q, k, v, g, x_in, gate_weight, gate_bias, lengths,
    dq_out, dk_out, dv_out, weight_out, bias_out,
    qh, kh, vh, gh, parts, part, logits, decay, starts,
    k_t, decay_col, score, grad, dk, dv, col, dq, row_sum, col_sum,
    halo_out, halo_in, low, cols_out, cols_in,
    gate, inbox, wide, term, stage, first, second, x, x_sem, saved_p, saved_s,
    in_send, in_recv, own_in, relay_send, relay_recv, small_send, small_recv,
    out_send, out_recv, own_out, halo_send, halo_recv,
    g_send, g_recv, z_send, z_recv, y_send, y_recv, w_send, w_recv,
):
    scale = HEAD ** (-0.5)
    home, window = RING * rows, RING * rows + HALO
    dp, tensor, y, ring = place()
    after, before = lax.rem(dp + RING, n_dp), lax.rem(dp + n_dp - RING, n_dp)
    plane = nz * RING
    xh = dp // plane
    z = lax.rem(dp, plane) // RING
    peers = [(ring_peer(dp, y, s), tensor) for s in range(1, RING)]
    mates = [(dp, lax.rem(tensor + s, n_tensor)) for s in range(1, n_tensor)]
    line = [(xh * plane + lax.rem(z + s, nz) * RING + y, tensor) for s in range(1, nz)]
    sides = [
        (lax.rem(xh + a, nx) * plane + z * RING + lax.rem(y + b, RING), tensor)
        for a in range(nx)
        for b in range(RING)
    ][1:]
    homes = [
        (ring_peer(dp, y, a), lax.rem(tensor + b, n_tensor)) for a in range(RING) for b in range(n_tensor)
    ][1:]
    x_copy = pltpu.make_async_copy(x_in, x, x_sem)
    x_copy.start()

    def meanwhile():
        x_copy.wait()
        part[...] = lax.dot_general(
            gate_weight[...], x[...], (((1,), (1,)), ((), ())), preferred_element_type=F32
        )

    greet(homes + line + sides[RING - 1 :] + [(after, tensor), (before, tensor)], meanwhile)

    def columns(shard, h):
        return pl.ds(pl.multiple_of(shard * (2 * HEAD) + h * HEAD, HEAD), HEAD)

    def shard_rows(shard, offset=0):
        return pl.ds(pl.multiple_of(offset + shard * rows, rows), rows)

    arrive, own = {}, {}

    def fetch(h, arrays):
        for a in arrays:
            src, dst, ahead = ((k, kh, HALO), (v, vh, HALO), (q, qh, 0), (g, gh, 0))[a]
            at = shard_rows(y, ahead)
            for s in (2, 1, 3):
                arrive[h, a, s] = send(
                    src.at[:, columns(lax.rem(y + s, RING), h)], dst.at[h, at],
                    (in_send, in_recv), h * 12 + a * 3 + s - 1, peers[s - 1],
                )
            own[h, a] = pltpu.make_async_copy(
                src.at[:, columns(y, h)], dst.at[h, at], own_in.at[h * 4 + a]
            )
            own[h, a].start()

    def arrived(h, arrays):
        for a in arrays:
            own[h, a].wait()
            for s in range(1, RING):
                arrive[h, a, s].wait()

    def relay(h, arrays):
        tail = pl.ds(home, HALO)
        return [
            send(ref.at[h, tail], ref.at[h, pl.ds(0, HALO)], (relay_send, relay_recv), h * 2 + a, (after, tensor))
            for a, ref in [(a, (kh, vh)[a]) for a in arrays]
        ]


    small = (small_send, small_recv)
    outs = [
        send(part.at[pl.ds(pl.multiple_of(mate[1] * 8, 8), 8)], parts.at[s], small, s, mate)
        for s, mate in enumerate(mates)
    ]
    fetch(0, (0,))
    eye = lax.broadcasted_iota(jnp.int32, (8, 8), 0) == lax.broadcasted_iota(jnp.int32, (8, 8), 1)
    bias = jnp.sum(
        jnp.where(eye, jnp.broadcast_to(gate_bias[...], (8, 8)), 0.0), axis=1, keepdims=True
    )
    for copy in outs:
        copy.wait()
    logit = part[pl.ds(pl.multiple_of(tensor * 8, 8), 8), :] + bias
    for s in range(n_tensor - 1):
        logit = logit + parts[s]
    logits[2 + y] = logit
    spread = [
        send(logits.at[2 + y], logits.at[2 + y], small, 3 + s, peer) for s, peer in enumerate(peers)
    ]
    fetch(0, (1, 2, 3))
    fetch(1, range(4))
    docs = lengths.shape[1]
    at_0 = lax.broadcasted_iota(jnp.int32, (docs, docs), 0)
    at_1 = lax.broadcasted_iota(jnp.int32, (docs, docs), 1)
    ends = jnp.sum(
        jnp.where(at_1 <= at_0, jnp.broadcast_to(lengths[...], (docs, docs)).astype(F32), 0.0),
        axis=1, keepdims=True,
    ).astype(jnp.int32)
    origin = ring * rows - HALO
    for c in range(home // 512):
        position = ring * rows + c * 512 + lax.broadcasted_iota(jnp.int32, (docs, 512), 1)
        begun = fold(jnp.where(ends <= position, ends, 0), jnp.maximum)
        starts[:, c * 512 : (c + 1) * 512] = jnp.broadcast_to(
            jnp.max(begun, axis=0, keepdims=True) - origin, (8, 512)
        )
    for copy in spread:
        copy.wait()
    ahead = send(logits.at[4:6], logits.at[0:2], small, 6, (after, tensor))
    for h in range(2):
        dk[h] = jnp.zeros((window, HEAD), F32)
        dv[h] = jnp.zeros((window, HEAD), F32)
        col[h] = jnp.zeros((window, HEAD), F32)
    arrived(0, (0, 1))
    relays = relay(0, (0, 1))
    ahead.wait()
    pieces = []
    for s in range(6):
        keep = logits[s]
        keep = -(jnp.maximum(-keep, 0.0) + jnp.log1p(jnp.exp(-jnp.abs(keep))))
        pieces += [keep[:, c * 128 : (c + 1) * 128] * LOG2E for c in range(rows // 128)]
    carry = jnp.zeros((8, 1), F32)
    for i, piece in enumerate(running(pieces, False)):
        decay[:, i * 128 : (i + 1) * 128] = piece + carry
        carry = carry + piece[:, 127:128]
    which = lax.broadcasted_iota(jnp.int32, (8, 512), 0)

    def prepare(h, part_of):
        for c in part_of:
            at = slice(c * 512, (c + 1) * 512)
            k_t[:, at] = kh[h, at, :].T
            mine = jnp.where(which == 2 * y + h, decay[:, at], 0.0)
            decay_col[at, :] = jnp.broadcast_to(jnp.sum(mine, axis=0, keepdims=True), (8, 512)).T

    def tiles(h, low_tile, high_tile, saved=None):
        def step(t, carry):
            tile_step(
                scale, qh.at[h], kh.at[h], vh.at[h], gh.at[h], k_t, decay_col, starts, score, grad,
                dk.at[h], dv.at[h], col.at[h], dq.at[h], row_sum.at[h], t, saved,
            )
            return carry

        lax.fori_loop(low_tile, high_tile, step, 0)

    def products(h, low_tile, high_tile, saved):
        def step(t, carry):
            tile_products(scale, qh.at[h], gh.at[h], k_t, dk.at[h], dv.at[h], dq.at[h], saved, t)
            return carry

        lax.fori_loop(low_tile, high_tile, step, 0)

    leave = []

    def give(src, dst, h, a, shards_of):
        def to(s):
            return pltpu.make_async_remote_copy(
                src_ref=src.at[shard_rows(lax.rem(y + s, RING))],
                dst_ref=dst.at[:, columns(y, h)],
                send_sem=out_send.at[h * 9 + a * 3 + s - 1],
                recv_sem=out_recv.at[h * 9 + a * 3 + s - 1],
                device_id=(ring_peer(dp, y, s), tensor),
                device_id_type=MESH,
            )

        copy = pltpu.make_async_copy(src.at[shard_rows(y)], dst.at[:, columns(y, h)], own_out.at[h * 3 + a])
        for s in (2, 1, 3):
            there = lax.rem(y + s, RING)
            pl.when((there >= shards_of[0]) & (there < shards_of[1]))(to(s).start)
        pl.when((y >= shards_of[0]) & (y < shards_of[1]))(copy.start)
        if shards_of[0] == 0:
            leave.extend([to(1), to(2), to(3), copy])

    back = {}

    def give_halo(h):
        halo_out[h, 0] = (dk[h, :HALO, :] * scale).astype(BF16)
        halo_out[h, 1] = dv[h, :HALO, :].astype(BF16)
        for a in range(2):
            back[h, a] = send(
                halo_out.at[h, a], halo_in.at[h, a], (halo_send, halo_recv), h * 2 + a, (before, tensor)
            )

    grads = ((dk, scale, dk_out), (dv, 1.0, dv_out))
    split = home - HALO
    near, far = (0, split // rows), (split // rows, RING)

    def cast_near(h):
        for a, (of, factor, _) in enumerate(grads):
            low[h, a, :split, :] = (of[h, HALO:home, :] * factor).astype(BF16)

    def give_near(h, arrays=(0, 1)):
        for a in arrays:
            out = grads[a][2]
            give(low.at[h, a], out, h, a + 1, near)

    def give_far(h):
        for a, (of, factor, out) in enumerate(grads):
            back[h, a].wait()
            low[h, a, split:, :] = (
                of[h, home:, :] * factor + halo_in[h, a].astype(F32)
            ).astype(BF16)
            give(low.at[h, a], out, h, a + 1, far)

    def sum_columns(h, at):
        col_sum[h, :, at] = lax.dot_general(
            jnp.ones((8, HEAD), F32), col[h, at], (((1,), (1,)), ((), ())),
            precision=lax.Precision.HIGHEST, preferred_element_type=F32,
        )

    behind, within = slice(0, HALO), slice(HALO, window)
    blocks = window // 512
    halo_blocks = HALO // 512
    half = HALO // TILE
    full = home // TILE
    prepare(0, range(halo_blocks, blocks))
    arrived(0, (2, 3))
    tiles(0, half, full)
    arrived(1, (0,))
    relays_1 = relay(1, (0,))
    for copy in relays:
        copy.wait()
    prepare(0, range(halo_blocks))
    tiles(0, 0, half // 2)
    arrived(1, (1,))
    relays_1 += relay(1, (1,))
    tiles(0, half // 2, half)
    give_halo(0)
    cast_near(0)
    give(dq.at[0], dq_out, 0, 0, (0, RING))
    give_near(0)
    sum_columns(0, behind)
    sum_columns(0, within)
    prepare(1, range(halo_blocks, blocks))
    arrived(1, (2, 3))
    saved = (saved_p, saved_s)
    for copy in relays_1:
        copy.wait()
    prepare(1, range(halo_blocks))
    tiles(1, 0, half, saved)

    sum_columns(1, behind)
    which = lax.broadcasted_iota(jnp.int32, (8, 128), 0)
    for c in range(HALO // 128):
        at = slice(c * 128, (c + 1) * 128)
        cols_out[:, at] = jnp.where(which == 0, col_sum[0, :, at], col_sum[1, :, at])
    cols = send(cols_out, cols_in, small, 7, (before, tensor))
    tiles(1, half, full, saved)
    sum_columns(1, within)

    pieces, falls = {}, {}
    for h in range(2):
        for c in range(home // 128):
            at = slice(c * 128, (c + 1) * 128)
            pieces[h, c] = row_sum[h, :, at] - col_sum[h, :, HALO + c * 128 : HALO + (c + 1) * 128]
            shard, off = divmod(c * 128, rows)
            raw = logits[2 + shard, :, off : off + 128]
            raw = jnp.sum(jnp.where(which == 2 * y + h, raw, 0.0), axis=0, keepdims=True)
            down = jnp.exp(-jnp.abs(raw))
            falls[h, c] = jnp.where(raw >= 0, down, 1.0) / (1.0 + down)
    sums = dict(zip(pieces, running(list(pieces.values()), True)))
    keeps = {}
    for h in range(2):
        carry = jnp.zeros((8, 1), F32)
        for c in reversed(range(home // 128)):
            keeps[h, c] = sums[h, c] + carry
            carry = carry + sums[h, c][:, 0:1]
    cols.wait()
    ahead_of = running([cols_in[:, c * 128 : (c + 1) * 128] for c in range(HALO // 128)], False)
    bias_sum = jnp.zeros((8, 1), F32)
    packed = {}
    before_it = jnp.zeros((8, 1), F32)
    share = {}
    for c in range(home // 128):
        if c * 128 < split:
            share[c] = jnp.zeros((8, 128), F32)
        else:
            i = (c * 128 - split) // 128
            share[c] = ahead_of[i] - cols_in[:, i * 128 : (i + 1) * 128] + before_it
            before_it = before_it + ahead_of[i][:, 127:128]
    for h in range(2):
        mine_of = jnp.zeros((8, 1), F32)
        for c in range(home // 128):
            shard, off = divmod(c * 128, rows)
            gate_grad = (keeps[h, c] + share[c][h : h + 1, :]) * falls[h, c]
            mine_of = mine_of + jnp.sum(gate_grad, axis=1, keepdims=True)
            row = h * (rows // 128) + off // 128
            packed[shard] = jnp.where(which == row, gate_grad, packed.get(shard, 0.0))
        bias_sum = jnp.where(which[:, :1] == 2 * y + h, mine_of, bias_sum)
    for shard in range(RING):
        gate[shard] = packed[shard].astype(BF16).astype(F32)

    slot = tensor * RING + y
    copies = [
        send(gate.at[lax.rem(device[0], RING)], inbox.at[slot], (g_send, g_recv), s, device)
        for s, device in enumerate(homes)
    ]
    give_far(0)
    products(1, 0, half, saved)
    give_halo(1)
    products(1, half, full, saved)
    give(dq.at[1], dq_out, 1, 0, (0, RING))
    cast_near(1)
    give_near(1, (0,))
    inbox[slot] = gate[y]
    for copy in copies:
        copy.wait()
    for s in range(n_tensor * RING):
        for r in range(8):
            h, c = divmod(r, rows // 128)
            wide[2 * s + h : 2 * s + h + 1, c * 128 : (c + 1) * 128] = inbox[s, r : r + 1, :]
    term[...] = jnp.dot(wide[...].astype(BF16), x[...], preferred_element_type=F32)
    for c in range(nz):
        stage[c, : term.shape[0], :] = term[:, c * 128 : (c + 1) * 128]
        stage[c, term.shape[0] :, :] = jnp.broadcast_to(bias_sum, (8, 128))
    heads = term.shape[0]
    parts_of = [pl.ds(0, heads // 2), pl.ds(heads // 2, heads // 2 + 8)]
    lanes = pl.ds(pl.multiple_of(z * 128, 128), 128)
    copies = [
        [
            send(
                stage.at[lax.rem(device[0], plane) // RING, part_of], first.at[s, part_of],
                (z_send, z_recv), i * len(line) + s, device,
            )
            for s, device in enumerate(line)
        ]
        for i, part_of in enumerate(parts_of)
    ]

    for i, part_of in enumerate(parts_of):
        piece = stage[z, part_of]
        for s, copy in enumerate(copies[i]):
            copy.wait()
            piece = piece + first[s, part_of]
        stage[z, part_of] = piece
        copies[i] = [
            send(stage.at[z, part_of], second.at[s, part_of], (y_send, y_recv), i * len(sides) + s, device)
            for s, device in enumerate(sides)
        ]
    give_near(1, (1,))
    give_far(1)

    for i, part_of in enumerate(parts_of):
        piece = stage[z, part_of]
        for s, copy in enumerate(copies[i]):
            copy.wait()
            piece = piece + second[s, part_of]
        at = pl.ds(i * (heads // 2), heads // 2)
        weight_out[at, lanes] = piece[: heads // 2]
        copies[i] = [
            send(weight_out.at[at, lanes], weight_out.at[at, lanes], (w_send, w_recv), i * len(line) + s, device)
            for s, device in enumerate(line)
        ]
    eye = which == lax.broadcasted_iota(jnp.int32, (8, 128), 1)
    bias_out[...] = jnp.sum(jnp.where(eye, piece[heads // 2 :], 0.0), axis=0, keepdims=True)[:, :8]
    for part in copies:
        for copy in part:
            copy.wait()
    for copy in leave:
        copy.wait()


def finish_kernel(*refs):
    count = len(refs) // 3
    ins, outs, held = refs[:count], refs[count : 2 * count], refs[2 * count : 3 * count]
    load, store = refs[3 * count :]
    pairs = []
    for i in range(count):
        rows = ins[i].shape[0]
        step = max(rows // 4, min(rows, 128))
        for r in range(0, rows, step):
            at, n = pl.ds(r, step), len(pairs)
            pairs.append((
                pltpu.make_async_copy(ins[i].at[at], held[i].at[at], load.at[n]),
                pltpu.make_async_copy(held[i].at[at], outs[i].at[at], store.at[n]),
            ))
    for copy, _ in pairs:
        copy.start()
    for copy, then in pairs:
        copy.wait()
        then.start()
    for _, then in pairs:
        then.wait()


def finish(*arrays):
    hbm = pl.BlockSpec(memory_space=pl.ANY)
    return pl.pallas_call(
        finish_kernel,
        out_shape=tuple(jax.ShapeDtypeStruct(a.shape, a.dtype) for a in arrays),
        in_specs=[hbm] * len(arrays),
        out_specs=(hbm,) * len(arrays),
        scratch_shapes=[pltpu.VMEM(a.shape, a.dtype) for a in arrays]
        + [pltpu.SemaphoreType.DMA((4 * len(arrays),))] * 2,
        compiler_params=pltpu.CompilerParams(vmem_limit_bytes=56 * 2**20),
        name="finish",
    )(*arrays)


def shards(n_dp, n_tensor, q, k, v, g, x, gate_weight, gate_bias, doc_lengths):
    rows, width = q.shape
    home, window = RING * rows, RING * rows + HALO
    heads = 8 * n_tensor
    nx = 2
    nz = n_dp // (RING * nx)
    assert width == 128 * nz and heads == 8 * RING and rows == 512
    chunks = BAND // TILE
    hbm, vmem = pl.BlockSpec(memory_space=pl.ANY), pl.BlockSpec(memory_space=pltpu.VMEM)

    def dma(*sizes):
        return [pltpu.SemaphoreType.DMA((size,)) for size in sizes]

    out = jax.ShapeDtypeStruct((rows, width), BF16)
    pair = [pltpu.VMEM((2, window, HEAD), F32)]
    dq, dk, dv, weight, bias = pl.pallas_call(
        functools.partial(main_kernel, rows, n_dp, n_tensor, nz, nx),
        out_shape=(
            out, out, out,
            jax.ShapeDtypeStruct((heads, width), F32),
            jax.ShapeDtypeStruct((1, 8), F32),
        ),
        in_specs=[hbm] * 5 + [vmem] * 3,
        out_specs=(hbm, hbm, hbm, vmem, vmem),
        scratch_shapes=[
            pltpu.VMEM((2, home, HEAD), BF16),
            pltpu.VMEM((2, window, HEAD), BF16),
            pltpu.VMEM((2, window, HEAD), BF16),
            pltpu.VMEM((2, home, HEAD), BF16),
            pltpu.VMEM((n_tensor - 1, 8, rows), F32),
            pltpu.VMEM((heads, rows), F32),
            pltpu.VMEM((6, 8, rows), F32),
            pltpu.VMEM((8, window), F32),
            pltpu.VMEM((8, home), jnp.int32),
            pltpu.VMEM((HEAD, window), BF16),
            pltpu.VMEM((window, 8), F32),
            pltpu.VMEM((chunks, TILE, TILE), F32),
            pltpu.VMEM((chunks, TILE, TILE), F32),
            *(pair * 3),
            pltpu.VMEM((2, home, HEAD), BF16),
            pltpu.VMEM((2, 8, home), F32),
            pltpu.VMEM((2, 8, window), F32),
            pltpu.VMEM((2, 2, HALO, HEAD), BF16),
            pltpu.VMEM((2, 2, HALO, HEAD), BF16),
            pltpu.VMEM((2, 2, home, HEAD), BF16),
            pltpu.VMEM((8, HALO), F32),
            pltpu.VMEM((8, HALO), F32),
            pltpu.VMEM((RING, 8, 128), F32),
            pltpu.VMEM((n_tensor * RING, 8, 128), F32),
            pltpu.VMEM((heads, rows), F32),
            pltpu.VMEM((heads, width), F32),
            pltpu.VMEM((nz, heads + 8, 128), F32),
            pltpu.VMEM((nz - 1, heads + 8, 128), F32),
            pltpu.VMEM((nx * RING - 1, heads + 8, 128), F32),
            pltpu.VMEM((rows, width), BF16),
            pltpu.SemaphoreType.DMA,
            *([pltpu.VMEM((home // TILE, chunks, TILE, TILE), BF16)] * 2),
            *dma(24, 24, 8, 4, 4, 8, 8),
            *dma(18, 18, 6, 4, 4),
            *dma(*[n_tensor * RING - 1] * 2, *[2 * nz - 2] * 2, *[2 * nx * RING - 2] * 2, *[2 * nz - 2] * 2),
        ],
        compiler_params=pltpu.CompilerParams(
            collective_id=0, has_side_effects=True, vmem_limit_bytes=56 * 2**20
        ),
        name="main",
    )(q, k, v, g, x, gate_weight.T, gate_bias.reshape(1, 8), doc_lengths.reshape(1, -1))
    dq, dk, dv, weight, bias = finish(dq, dk, dv, weight, bias)
    return dq, dk, dv, weight.T, bias.reshape(8)


def solution(mesh):
    return jax.shard_map(
        functools.partial(shards, mesh.shape["dp"], mesh.shape["tensor"]),
        mesh=mesh,
        in_specs=(
            P("dp", "tensor"),
            P("dp", "tensor"),
            P("dp", "tensor"),
            P("dp", "tensor"),
            P("dp", "tensor"),
            P("tensor", None),
            P("tensor"),
            P(),
        ),
        out_specs=(
            P("dp", "tensor"),
            P("dp", "tensor"),
            P("dp", "tensor"),
            P("tensor", None),
            P("tensor"),
        ),
        check_vma=False,
    )
```

```python
import functools
import math

import jax
import jax.numpy as jnp
from jax import lax
from jax.experimental import pallas as pl
from jax.experimental.pallas import tpu as pltpu
from jax.sharding import PartitionSpec as P

RING = 4
HALO = 1024
HEAD = 128
TILE = 256
BAND = HALO + TILE
LOG2E = math.log2(math.e)
DEAD = -1e30
MESH = pl.DeviceIdType.MESH
F32 = jnp.float32
BF16 = jnp.bfloat16


def place():
    dp, tensor = lax.axis_index("dp"), lax.axis_index("tensor")
    y = lax.rem(dp, RING)
    return dp, tensor, y, dp - y


def ring_peer(dp, y, step):
    return dp - y + lax.rem(y + step, RING)


def greet(devices, meanwhile):
    barrier = pltpu.get_barrier_semaphore()
    for device in devices:
        pl.semaphore_signal(barrier, inc=1, device_id=device, device_id_type=MESH)
    meanwhile()
    pl.semaphore_wait(barrier, len(devices))


def send(src, dst, sems, at, device):
    copy = pltpu.make_async_remote_copy(
        src_ref=src,
        dst_ref=dst,
        send_sem=sems[0].at[at],
        recv_sem=sems[1].at[at],
        device_id=device,
        device_id_type=MESH,
    )
    copy.start()
    return copy


def fold(x, combine):
    out = x[:8]
    for r in range(8, x.shape[0], 8):
        out = combine(out, x[r : r + 8])
    return out


def running(chunks, later):
    a = lax.broadcasted_iota(jnp.int32, (128, 128), 0)
    b = lax.broadcasted_iota(jnp.int32, (128, 128), 1)
    ones = jnp.where(a >= b if later else a <= b, 1.0, 0.0).astype(F32)
    sums = jnp.dot(
        jnp.concatenate(chunks), ones, precision=lax.Precision.HIGHEST, preferred_element_type=F32
    )
    return [sums[8 * i : 8 * i + 8] for i in range(len(chunks))]


def tile_step(scale, q, k, v, g, k_t, decay_col, starts, score, grad, dk, dv, col, dq, rows_sum, t, saved=None):
    chunks = BAND // TILE
    nt = (((1,), (1,)), ((), ()))
    base = pl.multiple_of(t * TILE, TILE)
    mine = pl.ds(base, TILE)
    q_t, g_t = q[mine, :], g[mine, :]
    first = starts[0:1, mine] - base
    key_at = lax.broadcasted_iota(jnp.int32, (TILE, TILE), 0)
    top = jnp.full((8, TILE), DEAD, F32)
    for c in range(chunks):
        at = pl.ds(base + c * TILE, TILE)
        s = lax.dot_general(k[at, :], q_t, nt, preferred_element_type=F32)
        s = s * (scale * LOG2E) - decay_col[at, 0:1]
        live = key_at >= first - c * TILE
        if c == chunks - 1:
            live = live & (key_at <= lax.broadcasted_iota(jnp.int32, (TILE, TILE), 1))
        s = jnp.where(live, s, DEAD)
        score[c] = s
        top = jnp.maximum(top, fold(s, jnp.maximum))
    top = jnp.max(top, axis=0, keepdims=True)
    total = jnp.zeros((8, TILE), F32)
    delta = jnp.zeros((8, TILE), F32)
    for c in range(chunks):
        at = pl.ds(base + c * TILE, TILE)
        w = jnp.exp2(score[c] - top)
        d = lax.dot_general(v[at, :], g_t, nt, preferred_element_type=F32)
        score[c] = w
        grad[c] = d
        total = total + fold(w, jnp.add)
        delta = delta + fold(w * d, jnp.add)
    total = jnp.sum(total, axis=0, keepdims=True)
    inverse = 1.0 / total
    delta = jnp.sum(delta, axis=0, keepdims=True) * inverse
    rows_sum[:, mine] = jnp.broadcast_to(delta - delta * (total * inverse), (8, TILE))
    dq_t = jnp.zeros((HEAD, TILE), F32)
    for c in range(chunks):
        at = pl.ds(base + c * TILE, TILE)
        p = score[c] * inverse
        ds = p * (grad[c] - delta)
        low = ds.astype(BF16)
        col[at, :] += ds[:, :HEAD] + ds[:, HEAD:]
        if saved is not None:
            saved[0][t, c] = p.astype(BF16)
            saved[1][t, c] = low
            continue
        dv[at, :] += jnp.dot(p.astype(BF16), g_t, preferred_element_type=F32)
        dk[at, :] += jnp.dot(low, q_t, preferred_element_type=F32)
        dq_t = dq_t + jnp.dot(k_t[:, at], low, preferred_element_type=F32)
    if saved is None:
        dq[mine, :] = (dq_t * scale).T.astype(BF16)


def tile_products(scale, q, g, k_t, dk, dv, dq, saved, t):
    base = pl.multiple_of(t * TILE, TILE)
    mine = pl.ds(base, TILE)
    q_t, g_t = q[mine, :], g[mine, :]
    dq_t = jnp.zeros((HEAD, TILE), F32)
    for c in range(BAND // TILE):
        at = pl.ds(base + c * TILE, TILE)
        low = saved[1][t, c]
        dv[at, :] += jnp.dot(saved[0][t, c], g_t, preferred_element_type=F32)
        dk[at, :] += jnp.dot(low, q_t, preferred_element_type=F32)
        dq_t = dq_t + jnp.dot(k_t[:, at], low, preferred_element_type=F32)
    dq[mine, :] = (dq_t * scale).T.astype(BF16)


def main_kernel(
    rows, n_dp, n_tensor, nz, nx,
    q, k, v, g, x_in, gate_weight, gate_bias, lengths,
    dq_out, dk_out, dv_out, weight_out, bias_out,
    qh, kh, vh, gh, parts, part, logits, decay, starts,
    k_t, decay_col, score, grad, dk, dv, col, dq, row_sum, col_sum,
    halo_out, halo_in, low, cols_out, cols_in,
    gate, inbox, wide, term, stage, first, second, x, x_sem, saved_p, saved_s,
    in_send, in_recv, own_in, relay_send, relay_recv, small_send, small_recv,
    out_send, out_recv, own_out, halo_send, halo_recv,
    g_send, g_recv, z_send, z_recv, y_send, y_recv, w_send, w_recv,
):
    scale = HEAD ** (-0.5)
    home, window = RING * rows, RING * rows + HALO
    dp, tensor, y, ring = place()
    after, before = lax.rem(dp + RING, n_dp), lax.rem(dp + n_dp - RING, n_dp)
    plane = nz * RING
    xh = dp // plane
    z = lax.rem(dp, plane) // RING
    peers = [(ring_peer(dp, y, s), tensor) for s in range(1, RING)]
    mates = [(dp, lax.rem(tensor + s, n_tensor)) for s in range(1, n_tensor)]
    line = [(xh * plane + lax.rem(z + s, nz) * RING + y, tensor) for s in range(1, nz)]
    sides = [
        (lax.rem(xh + a, nx) * plane + z * RING + lax.rem(y + b, RING), tensor)
        for a in range(nx)
        for b in range(RING)
    ][1:]
    homes = [
        (ring_peer(dp, y, a), lax.rem(tensor + b, n_tensor)) for a in range(RING) for b in range(n_tensor)
    ][1:]
    x_copy = pltpu.make_async_copy(x_in, x, x_sem)
    x_copy.start()

    def meanwhile():
        x_copy.wait()
        part[...] = lax.dot_general(
            gate_weight[...], x[...], (((1,), (1,)), ((), ())), preferred_element_type=F32
        )

    greet(homes + line + sides[RING - 1 :] + [(after, tensor), (before, tensor)], meanwhile)

    def columns(shard, h):
        return pl.ds(pl.multiple_of(shard * (2 * HEAD) + h * HEAD, HEAD), HEAD)

    def shard_rows(shard, offset=0):
        return pl.ds(pl.multiple_of(offset + shard * rows, rows), rows)

    arrive, own = {}, {}

    def fetch(h, arrays):
        for a in arrays:
            src, dst, ahead = ((k, kh, HALO), (v, vh, HALO), (q, qh, 0), (g, gh, 0))[a]
            at = shard_rows(y, ahead)
            for s in (2, 1, 3):
                arrive[h, a, s] = send(
                    src.at[:, columns(lax.rem(y + s, RING), h)], dst.at[h, at],
                    (in_send, in_recv), h * 12 + a * 3 + s - 1, peers[s - 1],
                )
            own[h, a] = pltpu.make_async_copy(
                src.at[:, columns(y, h)], dst.at[h, at], own_in.at[h * 4 + a]
            )
            own[h, a].start()

    def arrived(h, arrays):
        for a in arrays:
            own[h, a].wait()
            for s in range(1, RING):
                arrive[h, a, s].wait()

    def relay(h, arrays):
        tail = pl.ds(home, HALO)
        return [
            send(ref.at[h, tail], ref.at[h, pl.ds(0, HALO)], (relay_send, relay_recv), h * 2 + a, (after, tensor))
            for a, ref in [(a, (kh, vh)[a]) for a in arrays]
        ]


    small = (small_send, small_recv)
    outs = [
        send(part.at[pl.ds(pl.multiple_of(mate[1] * 8, 8), 8)], parts.at[s], small, s, mate)
        for s, mate in enumerate(mates)
    ]
    fetch(0, (0, 1))
    eye = lax.broadcasted_iota(jnp.int32, (8, 8), 0) == lax.broadcasted_iota(jnp.int32, (8, 8), 1)
    bias = jnp.sum(
        jnp.where(eye, jnp.broadcast_to(gate_bias[...], (8, 8)), 0.0), axis=1, keepdims=True
    )
    for copy in outs:
        copy.wait()
    logit = part[pl.ds(pl.multiple_of(tensor * 8, 8), 8), :] + bias
    for s in range(n_tensor - 1):
        logit = logit + parts[s]
    logits[2 + y] = logit
    spread = [
        send(logits.at[2 + y], logits.at[2 + y], small, 3 + s, peer) for s, peer in enumerate(peers)
    ]
    fetch(0, (2, 3))
    fetch(1, range(4))
    docs = lengths.shape[1]
    at_0 = lax.broadcasted_iota(jnp.int32, (docs, docs), 0)
    at_1 = lax.broadcasted_iota(jnp.int32, (docs, docs), 1)
    ends = jnp.sum(
        jnp.where(at_1 <= at_0, jnp.broadcast_to(lengths[...], (docs, docs)).astype(F32), 0.0),
        axis=1, keepdims=True,
    ).astype(jnp.int32)
    origin = ring * rows - HALO
    for c in range(home // 512):
        position = ring * rows + c * 512 + lax.broadcasted_iota(jnp.int32, (docs, 512), 1)
        begun = fold(jnp.where(ends <= position, ends, 0), jnp.maximum)
        starts[:, c * 512 : (c + 1) * 512] = jnp.broadcast_to(
            jnp.max(begun, axis=0, keepdims=True) - origin, (8, 512)
        )
    for copy in spread:
        copy.wait()
    ahead = send(logits.at[4:6], logits.at[0:2], small, 6, (after, tensor))
    for h in range(2):
        dk[h] = jnp.zeros((window, HEAD), F32)
        dv[h] = jnp.zeros((window, HEAD), F32)
        col[h] = jnp.zeros((window, HEAD), F32)
    arrived(0, (0, 1))
    relays = relay(0, (0, 1))
    ahead.wait()
    pieces = []
    for s in range(6):
        keep = logits[s]
        keep = -(jnp.maximum(-keep, 0.0) + jnp.log1p(jnp.exp(-jnp.abs(keep))))
        pieces += [keep[:, c * 128 : (c + 1) * 128] * LOG2E for c in range(rows // 128)]
    carry = jnp.zeros((8, 1), F32)
    for i, piece in enumerate(running(pieces, False)):
        decay[:, i * 128 : (i + 1) * 128] = piece + carry
        carry = carry + piece[:, 127:128]
    which = lax.broadcasted_iota(jnp.int32, (8, 512), 0)

    def prepare(h, part_of):
        for c in part_of:
            at = slice(c * 512, (c + 1) * 512)
            k_t[:, at] = kh[h, at, :].T
            mine = jnp.where(which == 2 * y + h, decay[:, at], 0.0)
            decay_col[at, :] = jnp.broadcast_to(jnp.sum(mine, axis=0, keepdims=True), (8, 512)).T

    def tiles(h, low_tile, high_tile, saved=None):
        def step(t, carry):
            tile_step(
                scale, qh.at[h], kh.at[h], vh.at[h], gh.at[h], k_t, decay_col, starts, score, grad,
                dk.at[h], dv.at[h], col.at[h], dq.at[h], row_sum.at[h], t, saved,
            )
            return carry

        lax.fori_loop(low_tile, high_tile, step, 0)

    def products(h, low_tile, high_tile, saved):
        def step(t, carry):
            tile_products(scale, qh.at[h], gh.at[h], k_t, dk.at[h], dv.at[h], dq.at[h], saved, t)
            return carry

        lax.fori_loop(low_tile, high_tile, step, 0)

    leave = []

    def give(src, dst, h, a, shards_of):
        def to(s):
            return pltpu.make_async_remote_copy(
                src_ref=src.at[shard_rows(lax.rem(y + s, RING))],
                dst_ref=dst.at[:, columns(y, h)],
                send_sem=out_send.at[h * 9 + a * 3 + s - 1],
                recv_sem=out_recv.at[h * 9 + a * 3 + s - 1],
                device_id=(ring_peer(dp, y, s), tensor),
                device_id_type=MESH,
            )

        copy = pltpu.make_async_copy(src.at[shard_rows(y)], dst.at[:, columns(y, h)], own_out.at[h * 3 + a])
        for s in (2, 1, 3):
            there = lax.rem(y + s, RING)
            pl.when((there >= shards_of[0]) & (there < shards_of[1]))(to(s).start)
        pl.when((y >= shards_of[0]) & (y < shards_of[1]))(copy.start)
        if shards_of[0] == 0:
            leave.extend([to(1), to(2), to(3), copy])

    back = {}

    def give_halo(h):
        halo_out[h, 0] = (dk[h, :HALO, :] * scale).astype(BF16)
        halo_out[h, 1] = dv[h, :HALO, :].astype(BF16)
        for a in range(2):
            back[h, a] = send(
                halo_out.at[h, a], halo_in.at[h, a], (halo_send, halo_recv), h * 2 + a, (before, tensor)
            )

    grads = ((dk, scale, dk_out), (dv, 1.0, dv_out))
    split = home - HALO
    near, far = (0, split // rows), (split // rows, RING)

    def cast_near(h):
        for a, (of, factor, _) in enumerate(grads):
            low[h, a, :split, :] = (of[h, HALO:home, :] * factor).astype(BF16)

    def give_near(h, arrays=(0, 1)):
        for a in arrays:
            out = grads[a][2]
            give(low.at[h, a], out, h, a + 1, near)

    def give_far(h):
        for a, (of, factor, out) in enumerate(grads):
            back[h, a].wait()
            low[h, a, split:, :] = (
                of[h, home:, :] * factor + halo_in[h, a].astype(F32)
            ).astype(BF16)
            give(low.at[h, a], out, h, a + 1, far)

    def sum_columns(h, at):
        col_sum[h, :, at] = lax.dot_general(
            jnp.ones((8, HEAD), F32), col[h, at], (((1,), (1,)), ((), ())),
            precision=lax.Precision.HIGHEST, preferred_element_type=F32,
        )

    behind, within = slice(0, HALO), slice(HALO, window)
    blocks = window // 512
    halo_blocks = HALO // 512
    half = HALO // TILE
    full = home // TILE
    prepare(0, range(halo_blocks, blocks))
    arrived(0, (2, 3))
    tiles(0, half, full)
    arrived(1, (0,))
    relays_1 = relay(1, (0,))
    for copy in relays:
        copy.wait()
    prepare(0, range(halo_blocks))
    tiles(0, 0, half // 2)
    arrived(1, (1,))
    relays_1 += relay(1, (1,))
    tiles(0, half // 2, half)
    give_halo(0)
    cast_near(0)
    give(dq.at[0], dq_out, 0, 0, (0, RING))
    give_near(0)
    sum_columns(0, behind)
    sum_columns(0, within)
    prepare(1, range(halo_blocks, blocks))
    arrived(1, (2, 3))
    saved = (saved_p, saved_s)
    for copy in relays_1:
        copy.wait()
    prepare(1, range(halo_blocks))
    tiles(1, 0, half, saved)

    sum_columns(1, behind)
    which = lax.broadcasted_iota(jnp.int32, (8, 128), 0)
    for c in range(HALO // 128):
        at = slice(c * 128, (c + 1) * 128)
        cols_out[:, at] = jnp.where(which == 0, col_sum[0, :, at], col_sum[1, :, at])
    cols = send(cols_out, cols_in, small, 7, (before, tensor))
    tiles(1, half, full, saved)
    sum_columns(1, within)

    pieces, falls = {}, {}
    for h in range(2):
        for c in range(home // 128):
            at = slice(c * 128, (c + 1) * 128)
            pieces[h, c] = row_sum[h, :, at] - col_sum[h, :, HALO + c * 128 : HALO + (c + 1) * 128]
            shard, off = divmod(c * 128, rows)
            raw = logits[2 + shard, :, off : off + 128]
            raw = jnp.sum(jnp.where(which == 2 * y + h, raw, 0.0), axis=0, keepdims=True)
            down = jnp.exp(-jnp.abs(raw))
            falls[h, c] = jnp.where(raw >= 0, down, 1.0) / (1.0 + down)
    sums = dict(zip(pieces, running(list(pieces.values()), True)))
    keeps = {}
    for h in range(2):
        carry = jnp.zeros((8, 1), F32)
        for c in reversed(range(home // 128)):
            keeps[h, c] = sums[h, c] + carry
            carry = carry + sums[h, c][:, 0:1]
    cols.wait()
    ahead_of = running([cols_in[:, c * 128 : (c + 1) * 128] for c in range(HALO // 128)], False)
    bias_sum = jnp.zeros((8, 1), F32)
    packed = {}
    before_it = jnp.zeros((8, 1), F32)
    share = {}
    for c in range(home // 128):
        if c * 128 < split:
            share[c] = jnp.zeros((8, 128), F32)
        else:
            i = (c * 128 - split) // 128
            share[c] = ahead_of[i] - cols_in[:, i * 128 : (i + 1) * 128] + before_it
            before_it = before_it + ahead_of[i][:, 127:128]
    for h in range(2):
        mine_of = jnp.zeros((8, 1), F32)
        for c in range(home // 128):
            shard, off = divmod(c * 128, rows)
            gate_grad = (keeps[h, c] + share[c][h : h + 1, :]) * falls[h, c]
            mine_of = mine_of + jnp.sum(gate_grad, axis=1, keepdims=True)
            row = h * (rows // 128) + off // 128
            packed[shard] = jnp.where(which == row, gate_grad, packed.get(shard, 0.0))
        bias_sum = jnp.where(which[:, :1] == 2 * y + h, mine_of, bias_sum)
    for shard in range(RING):
        gate[shard] = packed[shard].astype(BF16).astype(F32)

    slot = tensor * RING + y
    copies = [
        send(gate.at[lax.rem(device[0], RING)], inbox.at[slot], (g_send, g_recv), s, device)
        for s, device in enumerate(homes)
    ]
    give_far(0)
    products(1, 0, half, saved)
    give_halo(1)
    products(1, half, full, saved)
    give(dq.at[1], dq_out, 1, 0, (0, RING))
    cast_near(1)
    give_near(1, (0,))
    inbox[slot] = gate[y]
    for copy in copies:
        copy.wait()
    for s in range(n_tensor * RING):
        for r in range(8):
            h, c = divmod(r, rows // 128)
            wide[2 * s + h : 2 * s + h + 1, c * 128 : (c + 1) * 128] = inbox[s, r : r + 1, :]
    term[...] = jnp.dot(wide[...].astype(BF16), x[...], preferred_element_type=F32)
    for c in range(nz):
        stage[c, : term.shape[0], :] = term[:, c * 128 : (c + 1) * 128]
        stage[c, term.shape[0] :, :] = jnp.broadcast_to(bias_sum, (8, 128))
    heads = term.shape[0]
    parts_of = [pl.ds(0, heads // 2), pl.ds(heads // 2, heads // 2 + 8)]
    lanes = pl.ds(pl.multiple_of(z * 128, 128), 128)
    copies = [
        [
            send(
                stage.at[lax.rem(device[0], plane) // RING, part_of], first.at[s, part_of],
                (z_send, z_recv), i * len(line) + s, device,
            )
            for s, device in enumerate(line)
        ]
        for i, part_of in enumerate(parts_of)
    ]

    for i, part_of in enumerate(parts_of):
        piece = stage[z, part_of]
        for s, copy in enumerate(copies[i]):
            copy.wait()
            piece = piece + first[s, part_of]
        stage[z, part_of] = piece
        copies[i] = [
            send(stage.at[z, part_of], second.at[s, part_of], (y_send, y_recv), i * len(sides) + s, device)
            for s, device in enumerate(sides)
        ]
    give_near(1, (1,))
    give_far(1)

    for i, part_of in enumerate(parts_of):
        piece = stage[z, part_of]
        for s, copy in enumerate(copies[i]):
            copy.wait()
            piece = piece + second[s, part_of]
        at = pl.ds(i * (heads // 2), heads // 2)
        weight_out[at, lanes] = piece[: heads // 2]
        copies[i] = [
            send(weight_out.at[at, lanes], weight_out.at[at, lanes], (w_send, w_recv), i * len(line) + s, device)
            for s, device in enumerate(line)
        ]
    eye = which == lax.broadcasted_iota(jnp.int32, (8, 128), 1)
    bias_out[...] = jnp.sum(jnp.where(eye, piece[heads // 2 :], 0.0), axis=0, keepdims=True)[:, :8]
    for part in copies:
        for copy in part:
            copy.wait()
    for copy in leave:
        copy.wait()


def finish_kernel(*refs):
    count = len(refs) // 3
    ins, outs, held = refs[:count], refs[count : 2 * count], refs[2 * count : 3 * count]
    load, store = refs[3 * count :]
    pairs = []
    for i in range(count):
        rows = ins[i].shape[0]
        step = max(rows // 4, min(rows, 128))
        for r in range(0, rows, step):
            at, n = pl.ds(r, step), len(pairs)
            pairs.append((
                pltpu.make_async_copy(ins[i].at[at], held[i].at[at], load.at[n]),
                pltpu.make_async_copy(held[i].at[at], outs[i].at[at], store.at[n]),
            ))
    for copy, _ in pairs:
        copy.start()
    for copy, then in pairs:
        copy.wait()
        then.start()
    for _, then in pairs:
        then.wait()


def finish(*arrays):
    hbm = pl.BlockSpec(memory_space=pl.ANY)
    return pl.pallas_call(
        finish_kernel,
        out_shape=tuple(jax.ShapeDtypeStruct(a.shape, a.dtype) for a in arrays),
        in_specs=[hbm] * len(arrays),
        out_specs=(hbm,) * len(arrays),
        scratch_shapes=[pltpu.VMEM(a.shape, a.dtype) for a in arrays]
        + [pltpu.SemaphoreType.DMA((4 * len(arrays),))] * 2,
        compiler_params=pltpu.CompilerParams(vmem_limit_bytes=56 * 2**20),
        name="finish",
    )(*arrays)


def shards(n_dp, n_tensor, q, k, v, g, x, gate_weight, gate_bias, doc_lengths):
    rows, width = q.shape
    home, window = RING * rows, RING * rows + HALO
    heads = 8 * n_tensor
    nx = 2
    nz = n_dp // (RING * nx)
    assert width == 128 * nz and heads == 8 * RING and rows == 512
    chunks = BAND // TILE
    hbm, vmem = pl.BlockSpec(memory_space=pl.ANY), pl.BlockSpec(memory_space=pltpu.VMEM)

    def dma(*sizes):
        return [pltpu.SemaphoreType.DMA((size,)) for size in sizes]

    out = jax.ShapeDtypeStruct((rows, width), BF16)
    pair = [pltpu.VMEM((2, window, HEAD), F32)]
    dq, dk, dv, weight, bias = pl.pallas_call(
        functools.partial(main_kernel, rows, n_dp, n_tensor, nz, nx),
        out_shape=(
            out, out, out,
            jax.ShapeDtypeStruct((heads, width), F32),
            jax.ShapeDtypeStruct((1, 8), F32),
        ),
        in_specs=[hbm] * 5 + [vmem] * 3,
        out_specs=(hbm, hbm, hbm, vmem, vmem),
        scratch_shapes=[
            pltpu.VMEM((2, home, HEAD), BF16),
            pltpu.VMEM((2, window, HEAD), BF16),
            pltpu.VMEM((2, window, HEAD), BF16),
            pltpu.VMEM((2, home, HEAD), BF16),
            pltpu.VMEM((n_tensor - 1, 8, rows), F32),
            pltpu.VMEM((heads, rows), F32),
            pltpu.VMEM((6, 8, rows), F32),
            pltpu.VMEM((8, window), F32),
            pltpu.VMEM((8, home), jnp.int32),
            pltpu.VMEM((HEAD, window), BF16),
            pltpu.VMEM((window, 8), F32),
            pltpu.VMEM((chunks, TILE, TILE), F32),
            pltpu.VMEM((chunks, TILE, TILE), F32),
            *(pair * 3),
            pltpu.VMEM((2, home, HEAD), BF16),
            pltpu.VMEM((2, 8, home), F32),
            pltpu.VMEM((2, 8, window), F32),
            pltpu.VMEM((2, 2, HALO, HEAD), BF16),
            pltpu.VMEM((2, 2, HALO, HEAD), BF16),
            pltpu.VMEM((2, 2, home, HEAD), BF16),
            pltpu.VMEM((8, HALO), F32),
            pltpu.VMEM((8, HALO), F32),
            pltpu.VMEM((RING, 8, 128), F32),
            pltpu.VMEM((n_tensor * RING, 8, 128), F32),
            pltpu.VMEM((heads, rows), F32),
            pltpu.VMEM((heads, width), F32),
            pltpu.VMEM((nz, heads + 8, 128), F32),
            pltpu.VMEM((nz - 1, heads + 8, 128), F32),
            pltpu.VMEM((nx * RING - 1, heads + 8, 128), F32),
            pltpu.VMEM((rows, width), BF16),
            pltpu.SemaphoreType.DMA,
            *([pltpu.VMEM((home // TILE, chunks, TILE, TILE), BF16)] * 2),
            *dma(24, 24, 8, 4, 4, 8, 8),
            *dma(18, 18, 6, 4, 4),
            *dma(*[n_tensor * RING - 1] * 2, *[2 * nz - 2] * 2, *[2 * nx * RING - 2] * 2, *[2 * nz - 2] * 2),
        ],
        compiler_params=pltpu.CompilerParams(
            collective_id=0, has_side_effects=True, vmem_limit_bytes=56 * 2**20
        ),
        name="main",
    )(q, k, v, g, x, gate_weight.T, gate_bias.reshape(1, 8), doc_lengths.reshape(1, -1))
    dq, dk, dv, weight, bias = finish(dq, dk, dv, weight, bias)
    return dq, dk, dv, weight.T, bias.reshape(8)


def solution(mesh):
    return jax.shard_map(
        functools.partial(shards, mesh.shape["dp"], mesh.shape["tensor"]),
        mesh=mesh,
        in_specs=(
            P("dp", "tensor"),
            P("dp", "tensor"),
            P("dp", "tensor"),
            P("dp", "tensor"),
            P("dp", "tensor"),
            P("tensor", None),
            P("tensor"),
            P(),
        ),
        out_specs=(
            P("dp", "tensor"),
            P("dp", "tensor"),
            P("dp", "tensor"),
            P("tensor", None),
            P("tensor"),
        ),
        check_vma=False,
    )
```
